512 devices in a mesh: seq: 32 (over y_hi, x, core), dp: 16 (over z, y_lo).
Axes of the slice: x: 4, y: 8 (y_hi: 4, y_lo: 2; y = y_hi * 2 + y_lo), z: 8, core: 2. Of those that a mesh axis runs over, the one named last changes fastest.
Arguments:
- span_queries: bfloat16 [4096, 4096], P('seq', 'dp'), may hold values from -2.5 to 2.5
- output_grad: bfloat16 [4096, 4096], P('seq', 'dp'), may hold values from -6 to 6
- neighbour_keys: bfloat16 [16384, 4096], P('seq', 'dp'), may hold values from -2.5 to 2.5
- neighbour_states: bfloat16 [16384, 4096], P('seq', 'dp'), may hold values from -6 to 6
- encoder_queries: bfloat16 [16384, 4096], P('seq', 'dp'), may hold values from -2.5 to 2.5
- span_keys: bfloat16 [4096, 4096], P('seq', 'dp'), may hold values from -2.5 to 2.5
- span_values: bfloat16 [4096, 4096], P('seq', 'dp'), may hold values from -6 to 6
- norm_gain: float32 [4096], P('dp'), may hold values from 0.25 to 1.75
Outputs:
- query_grad: bfloat16 [4096, 4096], P('seq', 'dp')
- key_grad: bfloat16 [16384, 4096], P('seq', 'dp')
- state_grad: bfloat16 [16384, 4096], P('seq', 'dp')
- encoder_query_grad: bfloat16 [16384, 4096], P('seq', 'dp')
- span_key_grad: bfloat16 [4096, 4096], P('seq', 'dp')
- span_value_grad: bfloat16 [4096, 4096], P('seq', 'dp')
- gain_grad: float32 [4096], P('dp')
The draws below stay inside these ranges and needn't reach their ends.
All inputs are finite; a program needn't handle non-finite values.
Results may differ from the reference program's by a relative error of at most 0.0064.
Values may be sent and summed in bfloat16 or wider, within the bound.
A program may use at most 64 MiB of HBM per device.

```python
import jax
import jax.numpy as jnp
from jax import lax

H = 32
HD = 128
SPAN = 64
LENGTH = 4096
SPANS = 64
MEM = 256
NROWS = 16384
WIDTH = 4096


def shard_levels(rng, shape, pieces, low, top_value):
    loudness, own = 1.0, jax.random.fold_in(rng, 6)
    for position, shards_of in pieces:
        steps = jnp.exp(jax.random.uniform(jax.random.fold_in(own, position), (shards_of,), jnp.float32, low / len(pieces), top_value / len(pieces)))
        loudness = loudness * jnp.repeat(steps, shape[position] // shards_of).reshape([-1 if axis == position else 1 for axis in range(len(shape))])
    return loudness


def centred(rng, extent, spread, reach, pieces=(), kind=jnp.bfloat16):
    array = spread * jax.random.normal(rng, extent, jnp.float32)
    if pieces:
        array = array * shard_levels(rng, extent, pieces, -0.22, 0.18)
    return jnp.clip(array, -reach, reach).astype(kind)


def setup_inputs(seed: int = 0) -> dict:
    arg_keys = jax.random.split(jax.random.key(seed), 9)
    span_queries = centred(arg_keys[0], (LENGTH, WIDTH), 1.0, 2.5, ((0, 32), (1, 16)))
    output_grad = centred(arg_keys[1], (LENGTH, WIDTH), 1.0, 6.0, ((0, 32), (1, 16)))
    neighbour_keys = centred(arg_keys[2], (NROWS, WIDTH), 1.0, 2.5, ((0, 32), (1, 16)))
    neighbour_states = centred(arg_keys[3], (NROWS, WIDTH), 1.0, 6.0, ((0, 32), (1, 16)))
    encoder_queries = centred(arg_keys[4], (NROWS, WIDTH), 1.0, 2.5, ((0, 32), (1, 16)))
    span_keys = centred(arg_keys[5], (LENGTH, WIDTH), 1.0, 2.5, ((0, 32), (1, 16)))
    span_values = centred(arg_keys[6], (LENGTH, WIDTH), 1.0, 6.0, ((0, 32), (1, 16)))
    norm_gain = jnp.clip(1.0 + 0.15 * jax.random.normal(arg_keys[7], (WIDTH,), jnp.float32), 0.25, 1.75)
    return {"span_queries": span_queries, "output_grad": output_grad, "neighbour_keys": neighbour_keys, "neighbour_states": neighbour_states, "encoder_queries": encoder_queries, "span_keys": span_keys, "span_values": span_values, "norm_gain": norm_gain}


norm_eps = 1e-05

def reference(span_queries, output_grad, neighbour_keys, neighbour_states, encoder_queries, span_keys, span_values, norm_gain):
    score_scale = HD ** (-0.5)
    enc_q = encoder_queries.astype(jnp.float32).reshape(SPANS, MEM, H, HD)
    enc_k = span_keys.astype(jnp.float32).reshape(SPANS, SPAN, H, HD)
    enc_v = span_values.astype(jnp.float32).reshape(SPANS, SPAN, H, HD)
    enc_scores = jnp.einsum('cmhd,cthd->chmt', enc_q, enc_k) * score_scale
    enc_weights = jnp.exp(enc_scores)
    enc_weights = enc_weights / lax.optimization_barrier(jnp.sum(enc_weights, axis=-1, keepdims=True))
    enc_low = enc_weights.astype(jnp.bfloat16)
    attended = jnp.einsum('chmt,cthd->cmhd', enc_low.astype(jnp.float32), enc_v)
    encoded = (neighbour_states.astype(jnp.float32).reshape(SPANS, MEM, H, HD) + attended).reshape(NROWS, WIDTH)
    inverse = lax.rsqrt(lax.optimization_barrier(jnp.mean(encoded * encoded, axis=-1, keepdims=True)) + norm_eps)
    normed = (encoded * inverse * norm_gain).astype(jnp.bfloat16)
    pad_rows = jnp.zeros((SPAN - 1, WIDTH), jnp.bfloat16)
    shifted_q = jnp.concatenate([span_queries[SPAN - 1:], pad_rows], axis=0)
    shifted_g = jnp.concatenate([output_grad[SPAN - 1:], pad_rows], axis=0)
    query_blocks = shifted_q.astype(jnp.float32).reshape(SPANS, SPAN, H, HD)
    grad_blocks = shifted_g.astype(jnp.float32).reshape(SPANS, SPAN, H, HD)
    key_blocks = neighbour_keys.astype(jnp.float32).reshape(SPANS, MEM, H, HD)
    value_blocks = normed.astype(jnp.float32).reshape(SPANS, MEM, H, HD)
    scores = jnp.einsum('cqhd,cmhd->chqm', query_blocks, key_blocks) * score_scale
    weights = jnp.exp(scores)
    weights = weights / lax.optimization_barrier(jnp.sum(weights, axis=-1, keepdims=True))
    weights_low = weights.astype(jnp.bfloat16)
    d_weights = jnp.einsum('cqhd,cmhd->chqm', grad_blocks, value_blocks)
    delta_sum = lax.optimization_barrier(jnp.sum(weights * d_weights, axis=-1, keepdims=True))
    d_scores = (weights * (d_weights - delta_sum) * score_scale).astype(jnp.bfloat16).astype(jnp.float32)
    d_query = jnp.einsum('chqm,cmhd->cqhd', d_scores, key_blocks).reshape(LENGTH, WIDTH)
    query_grad = jnp.concatenate([jnp.zeros((SPAN - 1, WIDTH), jnp.float32), d_query[:LENGTH - SPAN + 1]], axis=0).astype(jnp.bfloat16)
    key_grad = jnp.einsum('chqm,cqhd->cmhd', d_scores, query_blocks).reshape(NROWS, WIDTH).astype(jnp.bfloat16)
    value_grad = jnp.einsum('chqm,cqhd->cmhd', weights_low.astype(jnp.float32), grad_blocks).reshape(NROWS, WIDTH)
    gain_grad = lax.optimization_barrier(jnp.sum(value_grad * encoded * inverse, axis=0))
    scaled_grad = value_grad * norm_gain
    grad_dot = lax.optimization_barrier(jnp.sum(scaled_grad * encoded, axis=-1, keepdims=True))
    state_grad = (inverse * (scaled_grad - encoded * grad_dot * inverse * inverse / WIDTH)).astype(jnp.bfloat16)
    back_rows = state_grad.astype(jnp.float32).reshape(SPANS, MEM, H, HD)
    d_enc_weights = jnp.einsum('cmhd,cthd->chmt', back_rows, enc_v)
    enc_delta = lax.optimization_barrier(jnp.sum(enc_weights * d_enc_weights, axis=-1, keepdims=True))
    d_enc_scores = (enc_weights * (d_enc_weights - enc_delta) * score_scale).astype(jnp.bfloat16).astype(jnp.float32)
    encoder_query_grad = jnp.einsum('chmt,cthd->cmhd', d_enc_scores, enc_k).reshape(NROWS, WIDTH).astype(jnp.bfloat16)
    span_key_grad = jnp.einsum('chmt,cmhd->cthd', d_enc_scores, enc_q).reshape(LENGTH, WIDTH).astype(jnp.bfloat16)
    span_value_grad = jnp.einsum('chmt,cmhd->cthd', enc_low.astype(jnp.float32), back_rows).reshape(LENGTH, WIDTH).astype(jnp.bfloat16)
    return (query_grad, key_grad, state_grad, encoder_query_grad, span_key_grad, span_value_grad, gain_grad)
```

```python
import functools

import jax
import jax.numpy as jnp
from jax import lax
from jax.experimental import pallas as pl
from jax.experimental.pallas import tpu as pltpu
from jax.sharding import PartitionSpec as P

HD = 128
SPAN = 64
MEM = 256
NORM_EPS = 1e-05
SCALE = HD ** (-0.5)
MESH = pl.DeviceIdType.MESH
F32 = jnp.float32
BF16 = jnp.bfloat16


def nt(a, b):
    return lax.dot_general(a, b, (((1,), (1,)), ((), ())), preferred_element_type=F32)


def nn(a, b):
    return lax.dot_general(a, b, (((1,), (0,)), ((), ())), preferred_element_type=F32)


def tn(a, b):
    return lax.dot_general(a, b, (((0,), (0,)), ((), ())), preferred_element_type=F32)


def two_heads(x):
    first = lax.broadcasted_iota(jnp.int32, x.shape, 1) < HD
    zero = jnp.zeros_like(x)
    return jnp.concatenate([jnp.where(first, x, zero), jnp.where(first, zero, x)], axis=0)


def diagonal(x):
    first = lax.broadcasted_iota(jnp.int32, (SPAN, 2 * HD), 1) < HD
    return jnp.where(first, x[:SPAN], x[SPAN:])


def half_sums(x, left):
    zero = jnp.zeros_like(x)
    first = jnp.sum(jnp.where(left, x, zero), axis=1, keepdims=True)
    last = jnp.sum(jnp.where(left, zero, x), axis=1, keepdims=True)
    return first, last


def kernel(
    n_seq, n_dp, inner, sq_h, og_h, nk_h, ns_h, eq_h, sk_h, sv_h, gain_h,
    qg_h, kg_h, sg_h, eqg_h, skg_h, svg_h, gg_h,
    sq, og, nk, ns, eq, sk, sv, gain,
    qg, kg, sg, eqg, skg, svg, gg,
    next_q, next_g, dq_out, dq_in, enc, enc_w, enc_low, val, weights,
    part_out, part_in, gain_out, gain_in, gain_out2, gain_in2,
    in_sem, out_sem, halo_send, halo_recv, back_send, back_recv,
    part_send, part_recv, gain_send, gain_recv, gain_send2, gain_recv2,
):
    seq, dp = lax.axis_index("seq"), lax.axis_index("dp")
    before = lax.rem(seq + n_seq - 1, n_seq)
    after = lax.rem(seq + 1, n_seq)
    outer = n_seq // inner
    block = lax.div(seq, inner)
    place = lax.rem(seq, inner)
    width = n_dp * 2 * HD

    dp_peers = [(seq, lax.rem(dp + k, n_dp)) for k in range(1, n_dp)]
    in_peers = [(block * inner + lax.rem(place + k, inner), dp) for k in range(1, inner)]
    out_peers = [(lax.rem(block + k, outer) * inner + place, dp) for k in range(1, outer)]
    barrier = pltpu.get_barrier_semaphore()
    peers = [(before, dp), (after, dp)] + dp_peers + in_peers + out_peers
    for peer in peers:
        pl.semaphore_signal(barrier, inc=1, device_id=peer, device_id_type=MESH)

    loads = {}
    for k, (name, src, dst) in enumerate([
        ("eq", eq_h, eq), ("sk", sk_h, sk), ("sv", sv_h, sv), ("ns", ns_h, ns),
        ("sq", sq_h, sq), ("og", og_h, og), ("nk", nk_h, nk), ("gain", gain_h, gain),
    ]):
        loads[name] = pltpu.make_async_copy(src, dst, in_sem.at[k])
        loads[name].start()

    pl.semaphore_wait(barrier, len(peers))

    halo = [
        pltpu.make_async_remote_copy(
            src_ref=src.at[pl.ds(0, SPAN)], dst_ref=dst, send_sem=halo_send.at[k], recv_sem=halo_recv.at[k],
            device_id=(before, dp), device_id_type=MESH)
        for k, (src, dst) in enumerate([(sq_h, next_q), (og_h, next_g)])
    ]
    for copy in halo:
        copy.start()

    left = lax.broadcasted_iota(jnp.int32, (MEM, 2 * SPAN), 1) < SPAN
    tiles = 2 * MEM // 8
    pick = (
        lax.broadcasted_iota(jnp.int32, (tiles, 8, 128), 2)
        == lax.broadcasted_iota(jnp.int32, (tiles, 8, 128), 0)
    )
    pick2 = (
        lax.broadcasted_iota(jnp.int32, (tiles, 8, 128), 2)
        == lax.broadcasted_iota(jnp.int32, (tiles, 8, 128), 0) + tiles
    )

    def fold(x):
        return jnp.sum(x[:, :HD] + x[:, HD:], axis=1, keepdims=True)

    loads["eq"].wait()
    loads["sk"].wait()
    loads["sv"].wait()
    loads["ns"].wait()
    squares = []
    for c in range(2):
        rows = pl.ds(c * MEM, MEM)
        keys = two_heads(sk[pl.ds(c * SPAN, SPAN), :])
        values = two_heads(sv[pl.ds(c * SPAN, SPAN), :])
        e = jnp.exp(nt(eq[rows, :], keys) * SCALE)
        first, last = half_sums(e, left)
        w = e * jnp.where(left, 1.0 / first, 1.0 / last)
        low = w.astype(BF16)
        enc_w[rows, :] = w
        enc_low[rows, :] = low
        x = ns[rows, :].astype(F32) + nn(low, values)
        enc[rows, :] = x
        squares.append(fold(x * x))

    loads["sq"].wait()
    loads["og"].wait()
    loads["nk"].wait()
    loads["gain"].wait()
    gains = gain[...].reshape(1, 2 * HD)
    last_row = lax.broadcasted_iota(jnp.int32, (SPAN, 2 * HD), 0) == SPAN - 1

    def tokens(c):
        if c == 0:
            return (
                jnp.where(last_row, sq[:SPAN, :], sq[SPAN:, :]),
                jnp.where(last_row, og[:SPAN, :], og[SPAN:, :]),
            )
        there = seq < n_seq - 1
        zero = jnp.zeros((SPAN, 2 * HD), BF16)
        return (
            jnp.where(last_row, sq[SPAN:, :], jnp.where(there, next_q[...], zero)),
            jnp.where(last_row, og[SPAN:, :], jnp.where(there, next_g[...], zero)),
        )

    pairs, dots = [], []
    for c in range(2):
        rows = pl.ds(c * MEM, MEM)
        if c == 1:
            for copy in halo:
                copy.wait_recv()
        q, g = tokens(c)
        q, g = two_heads(q), two_heads(g)
        pairs.append((q, g))
        e = jnp.exp(nt(nk[rows, :], q) * SCALE)
        w = e * (1.0 / jnp.sum(e, axis=0, keepdims=True))
        weights[rows, :] = w
        v = nn(w.astype(BF16), g)
        val[rows, :] = v
        dots.append(fold(v * gains * enc[rows, :]))

    def packed(parts, mask):
        whole = jnp.concatenate(parts, axis=0).reshape(tiles, 8, 1)
        return jnp.sum(jnp.where(mask, whole, 0.0), axis=0)

    mine = packed(squares, pick) + packed(dots, pick2)
    part_out[...] = mine
    part = [
        pltpu.make_async_remote_copy(
            src_ref=part_out, dst_ref=part_in.at[k], send_sem=part_send, recv_sem=part_recv,
            device_id=peer, device_id_type=MESH)
        for k, peer in enumerate(dp_peers)
    ]
    for copy in part:
        copy.start()
    pltpu.make_async_copy(part_in, part_in, part_recv).wait()
    totals = mine + jnp.sum(part_in[...], axis=0)
    inverse = lax.rsqrt(totals * (1.0 / width) + NORM_EPS)
    grad_dot = pltpu.roll(totals, tiles, 1)
    slope = grad_dot * inverse * inverse * inverse * (1.0 / width)

    def column(x):
        return jnp.sum(jnp.where(pick, x[None], 0.0), axis=2, keepdims=True).reshape(2 * MEM, 1)

    inverse, slope = column(inverse), column(slope)

    own = jnp.zeros((8, 2 * HD), F32)
    for c in range(2):
        rows = pl.ds(c * MEM, MEM)
        term = val[rows, :] * enc[rows, :] * inverse[c * MEM:(c + 1) * MEM]
        own = own + jnp.sum(term.reshape(MEM // 8, 8, 2 * HD), axis=0)
    own = jnp.sum(own, axis=0, keepdims=True)
    gain_out[...] = jnp.broadcast_to(own, (8, 2 * HD))
    sums = [
        pltpu.make_async_remote_copy(
            src_ref=gain_out, dst_ref=gain_in.at[k], send_sem=gain_send, recv_sem=gain_recv,
            device_id=peer, device_id_type=MESH)
        for k, peer in enumerate(in_peers)
    ]
    for copy in sums:
        copy.start()

    stores = []

    def store(src, dst):
        copy = pltpu.make_async_copy(src, dst, out_sem.at[len(stores)])
        copy.start()
        stores.append(copy)

    d_query = [None, None]
    for c in (1, 0):
        rows = pl.ds(c * MEM, MEM)
        q, g = pairs[c]
        normed = (enc[rows, :] * inverse[c * MEM:(c + 1) * MEM] * gains).astype(BF16)
        w = weights[rows, :]
        d_w = nt(normed, g)
        delta = jnp.sum(w * d_w, axis=0, keepdims=True)
        d_s = (w * (d_w - delta) * SCALE).astype(BF16)
        d_query[c] = diagonal(tn(d_s, nk[rows, :])).astype(BF16)
        if c == 1:
            dq_out[...] = d_query[c]
            back = pltpu.make_async_remote_copy(
                src_ref=dq_out, dst_ref=dq_in, send_sem=back_send, recv_sem=back_recv,
                device_id=(after, dp), device_id_type=MESH)
            back.start()
        kg[rows, :] = nn(d_s, q).astype(BF16)
    store(kg, kg_h)

    pltpu.make_async_copy(gain_in, gain_in, gain_recv).wait()
    own = gain_out[...] + jnp.sum(gain_in[...], axis=0)
    gain_out2[...] = own
    sums2 = [
        pltpu.make_async_remote_copy(
            src_ref=gain_out2, dst_ref=gain_in2.at[k], send_sem=gain_send2, recv_sem=gain_recv2,
            device_id=peer, device_id_type=MESH)
        for k, peer in enumerate(out_peers)
    ]
    for copy in sums2:
        copy.start()

    for c in range(2):
        rows = pl.ds(c * MEM, MEM)
        at = slice(c * MEM, (c + 1) * MEM)
        span = pl.ds(c * SPAN, SPAN)
        keys = two_heads(sk[span, :])
        values = two_heads(sv[span, :])
        s_grad = (inverse[at] * (val[rows, :] * gains) - enc[rows, :] * slope[at]).astype(BF16)
        sg[rows, :] = s_grad
        w = enc_w[rows, :]
        d_w = nt(s_grad, values)
        first, last = half_sums(w * d_w, left)
        d_s = (w * (d_w - jnp.where(left, first, last)) * SCALE).astype(BF16)
        eqg[rows, :] = nn(d_s, keys).astype(BF16)
        skg[span, :] = diagonal(tn(d_s, eq[rows, :])).astype(BF16)
        svg[span, :] = diagonal(tn(enc_low[rows, :], s_grad)).astype(BF16)
    store(sg, sg_h)
    store(eqg, eqg_h)
    store(skg, skg_h)
    store(svg, svg_h)

    pltpu.make_async_copy(gain_in2, gain_in2, gain_recv2).wait()
    own = gain_out2[...] + jnp.sum(gain_in2[...], axis=0)
    gg[...] = own[0:1, :].reshape(2 * HD)
    store(gg, gg_h)

    back.wait_recv()
    come = jnp.where(seq > 0, dq_in[...], jnp.zeros((SPAN, 2 * HD), BF16))
    qg[:SPAN, :] = jnp.where(last_row, d_query[0], come)
    qg[SPAN:, :] = jnp.where(last_row, d_query[1], d_query[0])
    store(qg, qg_h)

    for copy in halo + [back]:
        copy.wait_send()
    for copies, sem in ((part, part_send), (sums, gain_send), (sums2, gain_send2)):
        for copy in copies:
            copy.wait_send()
    for copy in stores:
        copy.wait()


def solution(mesh):
    n_seq, n_dp = mesh.shape["seq"], mesh.shape["dp"]
    inner = 8 if n_seq % 8 == 0 and n_seq > 8 else n_seq // 2
    outer = n_seq // inner

    def step(*args):
        rows, width = args[0].shape
        many = args[2].shape[0]
        small, large = (rows, width), (many, width)
        out_shapes = [small, large, large, large, small, small]
        vmem = pltpu.VMEM
        dma = pltpu.SemaphoreType.DMA
        hbm = pl.BlockSpec(memory_space=pltpu.HBM)
        return pl.pallas_call(
            functools.partial(kernel, n_seq, n_dp, inner),
            out_shape=[jax.ShapeDtypeStruct(s, BF16) for s in out_shapes]
            + [jax.ShapeDtypeStruct((width,), F32)],
            in_specs=[hbm] * 8,
            out_specs=[hbm] * 7,
            scratch_shapes=[
                vmem(small, BF16), vmem(small, BF16), vmem(large, BF16), vmem(large, BF16),
                vmem(large, BF16), vmem(small, BF16), vmem(small, BF16), vmem((width,), F32),
            ]
            + [vmem(s, BF16) for s in out_shapes]
            + [vmem((width,), F32)]
            + [vmem((SPAN, width), BF16)] * 4
            + [
                vmem(large, F32), vmem((many, 2 * SPAN), F32), vmem((many, 2 * SPAN), BF16),
                vmem(large, F32), vmem((many, 2 * SPAN), F32),
                vmem((8, 128), F32), vmem((n_dp - 1, 8, 128), F32),
                vmem((8, width), F32), vmem((inner - 1, 8, width), F32),
                vmem((8, width), F32), vmem((outer - 1, 8, width), F32),
                dma((8,)), dma((7,)), dma((2,)), dma((2,)), dma, dma,
                dma, dma, dma, dma, dma, dma,
            ],
            compiler_params=pltpu.CompilerParams(
                collective_id=0, has_side_effects=True, vmem_limit_bytes=63 * 1024 * 1024
            ),
        )(*args)

    return jax.shard_map(
        step,
        mesh=mesh,
        in_specs=(P("seq", "dp"),) * 7 + (P("dp"),),
        out_specs=(P("seq", "dp"),) * 6 + (P("dp"),),
        check_vma=False,
    )
```

```python
import functools

import jax
import jax.numpy as jnp
from jax import lax
from jax.experimental import pallas as pl
from jax.experimental.pallas import tpu as pltpu
from jax.sharding import PartitionSpec as P

HD = 128
SPAN = 64
MEM = 256
NORM_EPS = 1e-05
SCALE = HD ** (-0.5)
MESH = pl.DeviceIdType.MESH
F32 = jnp.float32
BF16 = jnp.bfloat16


def nt(a, b):
    return lax.dot_general(a, b, (((1,), (1,)), ((), ())), preferred_element_type=F32)


def nn(a, b):
    return lax.dot_general(a, b, (((1,), (0,)), ((), ())), preferred_element_type=F32)


def tn(a, b):
    return lax.dot_general(a, b, (((0,), (0,)), ((), ())), preferred_element_type=F32)


def two_heads(x):
    first = lax.broadcasted_iota(jnp.int32, x.shape, 1) < HD
    zero = jnp.zeros_like(x)
    return jnp.concatenate([jnp.where(first, x, zero), jnp.where(first, zero, x)], axis=0)


def diagonal(x):
    first = lax.broadcasted_iota(jnp.int32, (SPAN, 2 * HD), 1) < HD
    return jnp.where(first, x[:SPAN], x[SPAN:])


def half_sums(x, left):
    zero = jnp.zeros_like(x)
    first = jnp.sum(jnp.where(left, x, zero), axis=1, keepdims=True)
    last = jnp.sum(jnp.where(left, zero, x), axis=1, keepdims=True)
    return first, last


def kernel(
    n_seq, n_dp, inner, sq_h, og_h, nk_h, ns_h, eq_h, sk_h, sv_h, gain_h,
    qg, kg, sg, eqg, skg, svg, gg,
    sq, og, nk, ns, eq, sk, sv, gain,
    next_q, next_g, dq_out, dq_in, enc, enc_w, enc_low, val, weights,
    part_out, part_in, gain_out, gain_in, gain_out2, gain_in2,
    in_sem, halo_send, halo_recv, back_send, back_recv,
    part_send, part_recv, gain_send, gain_recv, gain_send2, gain_recv2,
):
    seq, dp = lax.axis_index("seq"), lax.axis_index("dp")
    before = lax.rem(seq + n_seq - 1, n_seq)
    after = lax.rem(seq + 1, n_seq)
    outer = n_seq // inner
    block = lax.div(seq, inner)
    place = lax.rem(seq, inner)
    width = n_dp * 2 * HD

    dp_peers = [(seq, lax.rem(dp + k, n_dp)) for k in range(1, n_dp)]
    in_peers = [(block * inner + lax.rem(place + k, inner), dp) for k in range(1, inner)]
    out_peers = [(lax.rem(block + k, outer) * inner + place, dp) for k in range(1, outer)]
    barrier = pltpu.get_barrier_semaphore()
    peers = [(before, dp), (after, dp)] + dp_peers + in_peers + out_peers
    for peer in peers:
        pl.semaphore_signal(barrier, inc=1, device_id=peer, device_id_type=MESH)

    loads = {}
    for k, (name, src, dst) in enumerate([
        ("eq", eq_h, eq), ("sk", sk_h, sk), ("sv", sv_h, sv), ("ns", ns_h, ns),
        ("sq", sq_h, sq), ("og", og_h, og), ("nk", nk_h, nk), ("gain", gain_h, gain),
    ]):
        loads[name] = pltpu.make_async_copy(src, dst, in_sem.at[k])
        loads[name].start()

    pl.semaphore_wait(barrier, len(peers))

    halo = [
        pltpu.make_async_remote_copy(
            src_ref=src.at[pl.ds(0, SPAN)], dst_ref=dst, send_sem=halo_send.at[k], recv_sem=halo_recv.at[k],
            device_id=(before, dp), device_id_type=MESH)
        for k, (src, dst) in enumerate([(sq_h, next_q), (og_h, next_g)])
    ]
    for copy in halo:
        copy.start()

    left = lax.broadcasted_iota(jnp.int32, (MEM, 2 * SPAN), 1) < SPAN
    tiles = 2 * MEM // 8
    pick = (
        lax.broadcasted_iota(jnp.int32, (tiles, 8, 128), 2)
        == lax.broadcasted_iota(jnp.int32, (tiles, 8, 128), 0)
    )
    pick2 = (
        lax.broadcasted_iota(jnp.int32, (tiles, 8, 128), 2)
        == lax.broadcasted_iota(jnp.int32, (tiles, 8, 128), 0) + tiles
    )

    def fold(x):
        return jnp.sum(x[:, :HD] + x[:, HD:], axis=1, keepdims=True)

    loads["eq"].wait()
    loads["sk"].wait()
    loads["sv"].wait()
    loads["ns"].wait()
    squares = []
    for c in range(2):
        rows = pl.ds(c * MEM, MEM)
        keys = two_heads(sk[pl.ds(c * SPAN, SPAN), :])
        values = two_heads(sv[pl.ds(c * SPAN, SPAN), :])
        e = jnp.exp(nt(eq[rows, :], keys) * SCALE)
        first, last = half_sums(e, left)
        w = e * jnp.where(left, 1.0 / first, 1.0 / last)
        low = w.astype(BF16)
        enc_w[rows, :] = w
        enc_low[rows, :] = low
        x = ns[rows, :].astype(F32) + nn(low, values)
        enc[rows, :] = x
        squares.append(fold(x * x))

    loads["sq"].wait()
    loads["og"].wait()
    loads["nk"].wait()
    loads["gain"].wait()
    gains = gain[...].reshape(1, 2 * HD)
    last_row = lax.broadcasted_iota(jnp.int32, (SPAN, 2 * HD), 0) == SPAN - 1

    def tokens(c):
        if c == 0:
            return (
                jnp.where(last_row, sq[:SPAN, :], sq[SPAN:, :]),
                jnp.where(last_row, og[:SPAN, :], og[SPAN:, :]),
            )
        there = seq < n_seq - 1
        zero = jnp.zeros((SPAN, 2 * HD), BF16)
        return (
            jnp.where(last_row, sq[SPAN:, :], jnp.where(there, next_q[...], zero)),
            jnp.where(last_row, og[SPAN:, :], jnp.where(there, next_g[...], zero)),
        )

    pairs, dots = [], []
    for c in range(2):
        rows = pl.ds(c * MEM, MEM)
        if c == 1:
            for copy in halo:
                copy.wait_recv()
        q, g = tokens(c)
        q, g = two_heads(q), two_heads(g)
        pairs.append((q, g))
        e = jnp.exp(nt(nk[rows, :], q) * SCALE)
        w = e * (1.0 / jnp.sum(e, axis=0, keepdims=True))
        weights[rows, :] = w
        v = nn(w.astype(BF16), g)
        val[rows, :] = v
        dots.append(fold(v * gains * enc[rows, :]))

    def packed(parts, mask):
        whole = jnp.concatenate(parts, axis=0).reshape(tiles, 8, 1)
        return jnp.sum(jnp.where(mask, whole, 0.0), axis=0)

    mine = packed(squares, pick) + packed(dots, pick2)
    part_out[...] = mine
    part = [
        pltpu.make_async_remote_copy(
            src_ref=part_out, dst_ref=part_in.at[k], send_sem=part_send, recv_sem=part_recv,
            device_id=peer, device_id_type=MESH)
        for k, peer in enumerate(dp_peers)
    ]
    for copy in part:
        copy.start()
    pltpu.make_async_copy(part_in, part_in, part_recv).wait()
    totals = mine + jnp.sum(part_in[...], axis=0)
    inverse = lax.rsqrt(totals * (1.0 / width) + NORM_EPS)
    grad_dot = pltpu.roll(totals, tiles, 1)
    slope = grad_dot * inverse * inverse * inverse * (1.0 / width)

    def column(x):
        return jnp.sum(jnp.where(pick, x[None], 0.0), axis=2, keepdims=True).reshape(2 * MEM, 1)

    inverse, slope = column(inverse), column(slope)

    own = jnp.zeros((8, 2 * HD), F32)
    for c in range(2):
        rows = pl.ds(c * MEM, MEM)
        term = val[rows, :] * enc[rows, :] * inverse[c * MEM:(c + 1) * MEM]
        own = own + jnp.sum(term.reshape(MEM // 8, 8, 2 * HD), axis=0)
    own = jnp.sum(own, axis=0, keepdims=True)
    gain_out[...] = jnp.broadcast_to(own, (8, 2 * HD))
    sums = [
        pltpu.make_async_remote_copy(
            src_ref=gain_out, dst_ref=gain_in.at[k], send_sem=gain_send, recv_sem=gain_recv,
            device_id=peer, device_id_type=MESH)
        for k, peer in enumerate(in_peers)
    ]
    for copy in sums:
        copy.start()

    d_query = [None, None]
    for c in (1, 0):
        rows = pl.ds(c * MEM, MEM)
        q, g = pairs[c]
        normed = (enc[rows, :] * inverse[c * MEM:(c + 1) * MEM] * gains).astype(BF16)
        w = weights[rows, :]
        d_w = nt(normed, g)
        delta = jnp.sum(w * d_w, axis=0, keepdims=True)
        d_s = (w * (d_w - delta) * SCALE).astype(BF16)
        d_query[c] = diagonal(tn(d_s, nk[rows, :])).astype(BF16)
        if c == 1:
            dq_out[...] = d_query[c]
            back = pltpu.make_async_remote_copy(
                src_ref=dq_out, dst_ref=dq_in, send_sem=back_send, recv_sem=back_recv,
                device_id=(after, dp), device_id_type=MESH)
            back.start()
        kg[rows, :] = nn(d_s, q).astype(BF16)

    pltpu.make_async_copy(gain_in, gain_in, gain_recv).wait()
    own = gain_out[...] + jnp.sum(gain_in[...], axis=0)
    gain_out2[...] = own
    sums2 = [
        pltpu.make_async_remote_copy(
            src_ref=gain_out2, dst_ref=gain_in2.at[k], send_sem=gain_send2, recv_sem=gain_recv2,
            device_id=peer, device_id_type=MESH)
        for k, peer in enumerate(out_peers)
    ]
    for copy in sums2:
        copy.start()

    for c in range(2):
        rows = pl.ds(c * MEM, MEM)
        at = slice(c * MEM, (c + 1) * MEM)
        span = pl.ds(c * SPAN, SPAN)
        keys = two_heads(sk[span, :])
        values = two_heads(sv[span, :])
        s_grad = (inverse[at] * (val[rows, :] * gains) - enc[rows, :] * slope[at]).astype(BF16)
        sg[rows, :] = s_grad
        w = enc_w[rows, :]
        d_w = nt(s_grad, values)
        first, last = half_sums(w * d_w, left)
        d_s = (w * (d_w - jnp.where(left, first, last)) * SCALE).astype(BF16)
        eqg[rows, :] = nn(d_s, keys).astype(BF16)
        skg[span, :] = diagonal(tn(d_s, eq[rows, :])).astype(BF16)
        svg[span, :] = diagonal(tn(enc_low[rows, :], s_grad)).astype(BF16)

    pltpu.make_async_copy(gain_in2, gain_in2, gain_recv2).wait()
    own = gain_out2[...] + jnp.sum(gain_in2[...], axis=0)
    gg[...] = own[0:1, :].reshape(2 * HD)

    back.wait_recv()
    come = jnp.where(seq > 0, dq_in[...], jnp.zeros((SPAN, 2 * HD), BF16))
    qg[:SPAN, :] = jnp.where(last_row, d_query[0], come)
    qg[SPAN:, :] = jnp.where(last_row, d_query[1], d_query[0])

    for copy in halo + [back]:
        copy.wait_send()
    for copy in part + sums + sums2:
        copy.wait_send()


def write_back(*refs):
    sources, targets, sem = refs[:7], refs[7:14], refs[14]
    copies = [pltpu.make_async_copy(a, b, sem.at[k]) for k, (a, b) in enumerate(zip(sources, targets))]
    for copy in copies:
        copy.start()
    for copy in copies:
        copy.wait()


def solution(mesh):
    n_seq, n_dp = mesh.shape["seq"], mesh.shape["dp"]
    inner = 8 if n_seq % 8 == 0 and n_seq > 8 else n_seq // 2
    outer = n_seq // inner

    def step(*args):
        rows, width = args[0].shape
        many = args[2].shape[0]
        small, large = (rows, width), (many, width)
        out_shapes = [small, large, large, large, small, small]
        vmem = pltpu.VMEM
        dma = pltpu.SemaphoreType.DMA
        hbm = pl.BlockSpec(memory_space=pltpu.HBM)
        on_chip = pl.BlockSpec(memory_space=pltpu.VMEM)
        results = pl.pallas_call(
            functools.partial(kernel, n_seq, n_dp, inner),
            out_shape=[vmem(s, BF16) for s in out_shapes] + [vmem((width,), F32)],
            in_specs=[hbm] * 8,
            out_specs=[on_chip] * 7,
            scratch_shapes=[
                vmem(small, BF16), vmem(small, BF16), vmem(large, BF16), vmem(large, BF16),
                vmem(large, BF16), vmem(small, BF16), vmem(small, BF16), vmem((width,), F32),
            ]
            + [vmem((SPAN, width), BF16)] * 4
            + [
                vmem(large, F32), vmem((many, 2 * SPAN), F32), vmem((many, 2 * SPAN), BF16),
                vmem(large, F32), vmem((many, 2 * SPAN), F32),
                vmem((8, 128), F32), vmem((n_dp - 1, 8, 128), F32),
                vmem((8, width), F32), vmem((inner - 1, 8, width), F32),
                vmem((8, width), F32), vmem((outer - 1, 8, width), F32),
                dma((8,)), dma((2,)), dma((2,)), dma, dma,
                dma, dma, dma, dma, dma, dma,
            ],
            compiler_params=pltpu.CompilerParams(
                collective_id=0, has_side_effects=True, vmem_limit_bytes=58 * 1024 * 1024
            ),
        )(*args)
        return pl.pallas_call(
            write_back,
            out_shape=[jax.ShapeDtypeStruct(s, BF16) for s in out_shapes]
            + [jax.ShapeDtypeStruct((width,), F32)],
            in_specs=[pl.BlockSpec(memory_space=pl.ANY)] * 7,
            out_specs=[hbm] * 7,
            scratch_shapes=[dma((7,))],
        )(*[pltpu.with_memory_space_constraint(x, pltpu.VMEM) for x in results])

    return jax.shard_map(
        step,
        mesh=mesh,
        in_specs=(P("seq", "dp"),) * 7 + (P("dp"),),
        out_specs=(P("seq", "dp"),) * 6 + (P("dp"),),
        check_vma=False,
    )
```

```python
import functools

import jax
import jax.numpy as jnp
from jax import lax
from jax.experimental import pallas as pl
from jax.experimental.pallas import tpu as pltpu
from jax.sharding import PartitionSpec as P

HD = 128
SPAN = 64
MEM = 256
NORM_EPS = 1e-05
SCALE = HD ** (-0.5)
MESH = pl.DeviceIdType.MESH
F32 = jnp.float32
BF16 = jnp.bfloat16


def nt(a, b):
    return lax.dot_general(a, b, (((1,), (1,)), ((), ())), preferred_element_type=F32)


def nn(a, b):
    return lax.dot_general(a, b, (((1,), (0,)), ((), ())), preferred_element_type=F32)


def tn(a, b):
    return lax.dot_general(a, b, (((0,), (0,)), ((), ())), preferred_element_type=F32)


def two_heads(x):
    first = lax.broadcasted_iota(jnp.int32, x.shape, 1) < HD
    zero = jnp.zeros_like(x)
    return jnp.concatenate([jnp.where(first, x, zero), jnp.where(first, zero, x)], axis=0)


def diagonal(x):
    first = lax.broadcasted_iota(jnp.int32, (SPAN, 2 * HD), 1) < HD
    return jnp.where(first, x[:SPAN], x[SPAN:])


def half_sums(x, left):
    zero = jnp.zeros_like(x)
    first = jnp.sum(jnp.where(left, x, zero), axis=1, keepdims=True)
    last = jnp.sum(jnp.where(left, zero, x), axis=1, keepdims=True)
    return first, last


def kernel(
    n_seq, n_dp, inner, sq_h, og_h, nk_h, ns_h, eq_h, sk_h, sv_h, gain_h,
    qg, kg, sg, eqg, skg, svg, gg,
    sq, og, nk, ns, eq, sk, sv, gain,
    next_q, next_g, dq_out, dq_in, enc, enc_w, enc_low, val, weights,
    square_out, square_in, dot_out, dot_in, gain_out, gain_in, gain_out2, gain_in2,
    in_sem, halo_send, halo_recv, back_send, back_recv,
    square_send, square_recv, dot_send, dot_recv, gain_send, gain_recv, gain_send2, gain_recv2,
):
    seq, dp = lax.axis_index("seq"), lax.axis_index("dp")
    before = lax.rem(seq + n_seq - 1, n_seq)
    after = lax.rem(seq + 1, n_seq)
    outer = n_seq // inner
    block = lax.div(seq, inner)
    place = lax.rem(seq, inner)
    width = n_dp * 2 * HD

    far = sorted(range(1, n_dp), key=lambda k: -min(k, n_dp - k))
    dp_peers = [(seq, lax.rem(dp + k, n_dp)) for k in far]
    in_peers = [(block * inner + lax.rem(place + k, inner), dp) for k in range(1, inner)]
    out_peers = [(lax.rem(block + k, outer) * inner + place, dp) for k in range(1, outer)]
    barrier = pltpu.get_barrier_semaphore()
    peers = [(before, dp), (after, dp)] + dp_peers + out_peers + in_peers
    for peer in peers:
        pl.semaphore_signal(barrier, inc=1, device_id=peer, device_id_type=MESH)

    loads = {}
    for k, (name, src, dst) in enumerate([
        ("eq", eq_h, eq), ("sk", sk_h, sk), ("sv", sv_h, sv), ("ns", ns_h, ns),
        ("sq", sq_h, sq), ("og", og_h, og), ("nk", nk_h, nk), ("gain", gain_h, gain),
    ]):
        loads[name] = pltpu.make_async_copy(src, dst, in_sem.at[k])
        loads[name].start()

    left = lax.broadcasted_iota(jnp.int32, (MEM, 2 * SPAN), 1) < SPAN
    tiles = 2 * MEM // 8
    pick = (
        lax.broadcasted_iota(jnp.int32, (tiles, 8, 128), 2)
        == lax.broadcasted_iota(jnp.int32, (tiles, 8, 128), 0)
    )
    def fold(x):
        return jnp.sum(x[:, :HD] + x[:, HD:], axis=1, keepdims=True)

    loads["eq"].wait()
    loads["sk"].wait()
    loads["sv"].wait()
    loads["ns"].wait()
    squares = []
    for c in range(2):
        rows = pl.ds(c * MEM, MEM)
        keys = two_heads(sk[pl.ds(c * SPAN, SPAN), :])
        values = two_heads(sv[pl.ds(c * SPAN, SPAN), :])
        e = jnp.exp(nt(eq[rows, :], keys) * SCALE)
        first, last = half_sums(e, left)
        w = e * jnp.where(left, 1.0 / first, 1.0 / last)
        low = w.astype(BF16)
        enc_w[rows, :] = w
        enc_low[rows, :] = low
        x = ns[rows, :].astype(F32) + nn(low, values)
        enc[rows, :] = x
        squares.append(fold(x * x))

    def packed(parts):
        whole = jnp.concatenate(parts, axis=0).reshape(tiles, 8, 1)
        return jnp.sum(jnp.where(pick, whole, 0.0), axis=0)

    def column(x):
        return jnp.sum(jnp.where(pick, x[None], 0.0), axis=2, keepdims=True).reshape(2 * MEM, 1)

    def exchange(mine, out, into, send, recv):
        out[...] = mine
        copies = [
            pltpu.make_async_remote_copy(
                src_ref=out, dst_ref=into.at[k], send_sem=send, recv_sem=recv,
                device_id=peer, device_id_type=MESH)
            for k, peer in enumerate(dp_peers)
        ]
        for copy in copies:
            copy.start()
        return copies

    def gather(out, into, recv):
        pltpu.make_async_copy(into, into, recv).wait()
        return out[...] + jnp.sum(into[...], axis=0)

    squares = packed(squares)
    pl.semaphore_wait(barrier, len(peers))

    halo = [
        pltpu.make_async_remote_copy(
            src_ref=src.at[pl.ds(0, SPAN)], dst_ref=dst, send_sem=halo_send.at[k], recv_sem=halo_recv.at[k],
            device_id=(before, dp), device_id_type=MESH)
        for k, (src, dst) in enumerate([(sq_h, next_q), (og_h, next_g)])
    ]
    for copy in halo:
        copy.start()

    send_squares = exchange(squares, square_out, square_in, square_send, square_recv)

    loads["sq"].wait()
    loads["og"].wait()
    loads["nk"].wait()
    loads["gain"].wait()
    gains = gain[...].reshape(1, 2 * HD)
    last_row = lax.broadcasted_iota(jnp.int32, (SPAN, 2 * HD), 0) == SPAN - 1

    def tokens(c):
        if c == 0:
            return (
                jnp.where(last_row, sq[:SPAN, :], sq[SPAN:, :]),
                jnp.where(last_row, og[:SPAN, :], og[SPAN:, :]),
            )
        there = seq < n_seq - 1
        zero = jnp.zeros((SPAN, 2 * HD), BF16)
        return (
            jnp.where(last_row, sq[SPAN:, :], jnp.where(there, next_q[...], zero)),
            jnp.where(last_row, og[SPAN:, :], jnp.where(there, next_g[...], zero)),
        )

    pairs, dots = [], []
    for c in range(2):
        rows = pl.ds(c * MEM, MEM)
        if c == 1:
            for copy in halo:
                copy.wait_recv()
        q, g = tokens(c)
        q, g = two_heads(q), two_heads(g)
        pairs.append((q, g))
        e = jnp.exp(nt(nk[rows, :], q) * SCALE)
        w = e * (1.0 / jnp.sum(e, axis=0, keepdims=True))
        weights[rows, :] = w
        v = nn(w.astype(BF16), g)
        val[rows, :] = v
        dots.append(fold(v * gains * enc[rows, :]))

    send_dots = exchange(packed(dots), dot_out, dot_in, dot_send, dot_recv)
    inverse = lax.rsqrt(gather(square_out, square_in, square_recv) * (1.0 / width) + NORM_EPS)
    packed_inverse = inverse
    inverse = column(inverse)

    own = jnp.zeros((8, 2 * HD), F32)
    for c in range(2):
        rows = pl.ds(c * MEM, MEM)
        term = val[rows, :] * enc[rows, :] * inverse[c * MEM:(c + 1) * MEM]
        own = own + jnp.sum(term.reshape(MEM // 8, 8, 2 * HD), axis=0)
    own = jnp.sum(own, axis=0, keepdims=True)
    gain_out[...] = jnp.broadcast_to(own, (8, 2 * HD))
    sums = [
        pltpu.make_async_remote_copy(
            src_ref=gain_out, dst_ref=gain_in.at[k], send_sem=gain_send, recv_sem=gain_recv,
            device_id=peer, device_id_type=MESH)
        for k, peer in enumerate(in_peers)
    ]
    for copy in sums:
        copy.start()

    d_query = [None, None]
    for c in (1, 0):
        rows = pl.ds(c * MEM, MEM)
        q, g = pairs[c]
        normed = (enc[rows, :] * inverse[c * MEM:(c + 1) * MEM] * gains).astype(BF16)
        w = weights[rows, :]
        d_w = nt(normed, g)
        delta = jnp.sum(w * d_w, axis=0, keepdims=True)
        d_s = (w * (d_w - delta) * SCALE).astype(BF16)
        d_query[c] = diagonal(tn(d_s, nk[rows, :])).astype(BF16)
        if c == 1:
            dq_out[...] = d_query[c]
            back = pltpu.make_async_remote_copy(
                src_ref=dq_out, dst_ref=dq_in, send_sem=back_send, recv_sem=back_recv,
                device_id=(after, dp), device_id_type=MESH)
            back.start()
        kg[rows, :] = nn(d_s, q).astype(BF16)

    pltpu.make_async_copy(gain_in, gain_in, gain_recv).wait()
    own = gain_out[...] + jnp.sum(gain_in[...], axis=0)
    gain_out2[...] = own
    sums2 = [
        pltpu.make_async_remote_copy(
            src_ref=gain_out2, dst_ref=gain_in2.at[k], send_sem=gain_send2, recv_sem=gain_recv2,
            device_id=peer, device_id_type=MESH)
        for k, peer in enumerate(out_peers)
    ]
    for copy in sums2:
        copy.start()

    grad_dot = gather(dot_out, dot_in, dot_recv)
    slope = column(grad_dot * packed_inverse * packed_inverse * packed_inverse * (1.0 / width))
    for c in range(2):
        rows = pl.ds(c * MEM, MEM)
        at = slice(c * MEM, (c + 1) * MEM)
        span = pl.ds(c * SPAN, SPAN)
        keys = two_heads(sk[span, :])
        values = two_heads(sv[span, :])
        s_grad = (inverse[at] * (val[rows, :] * gains) - enc[rows, :] * slope[at]).astype(BF16)
        sg[rows, :] = s_grad
        w = enc_w[rows, :]
        d_w = nt(s_grad, values)
        first, last = half_sums(w * d_w, left)
        d_s = (w * (d_w - jnp.where(left, first, last)) * SCALE).astype(BF16)
        eqg[rows, :] = nn(d_s, keys).astype(BF16)
        skg[span, :] = diagonal(tn(d_s, eq[rows, :])).astype(BF16)
        svg[span, :] = diagonal(tn(enc_low[rows, :], s_grad)).astype(BF16)

    pltpu.make_async_copy(gain_in2, gain_in2, gain_recv2).wait()
    own = gain_out2[...] + jnp.sum(gain_in2[...], axis=0)
    gg[...] = own[0:1, :].reshape(2 * HD)

    back.wait_recv()
    come = jnp.where(seq > 0, dq_in[...], jnp.zeros((SPAN, 2 * HD), BF16))
    qg[:SPAN, :] = jnp.where(last_row, d_query[0], come)
    qg[SPAN:, :] = jnp.where(last_row, d_query[1], d_query[0])

    for copy in halo + [back]:
        copy.wait_send()
    for copy in send_squares + send_dots + sums + sums2:
        copy.wait_send()


def write_back(*refs):
    sources, targets, sem = refs[:7], refs[7:14], refs[14]
    copies = [pltpu.make_async_copy(a, b, sem.at[k]) for k, (a, b) in enumerate(zip(sources, targets))]
    for copy in copies:
        copy.start()
    for copy in copies:
        copy.wait()


def solution(mesh):
    n_seq, n_dp = mesh.shape["seq"], mesh.shape["dp"]
    inner = 8 if n_seq % 8 == 0 and n_seq > 8 else n_seq // 2
    outer = n_seq // inner

    def step(*args):
        rows, width = args[0].shape
        many = args[2].shape[0]
        small, large = (rows, width), (many, width)
        out_shapes = [small, large, large, large, small, small]
        vmem = pltpu.VMEM
        dma = pltpu.SemaphoreType.DMA
        hbm = pl.BlockSpec(memory_space=pltpu.HBM)
        on_chip = pl.BlockSpec(memory_space=pltpu.VMEM)
        results = pl.pallas_call(
            functools.partial(kernel, n_seq, n_dp, inner),
            out_shape=[vmem(s, BF16) for s in out_shapes] + [vmem((width,), F32)],
            in_specs=[hbm] * 8,
            out_specs=[on_chip] * 7,
            scratch_shapes=[
                vmem(small, BF16), vmem(small, BF16), vmem(large, BF16), vmem(large, BF16),
                vmem(large, BF16), vmem(small, BF16), vmem(small, BF16), vmem((width,), F32),
            ]
            + [vmem((SPAN, width), BF16)] * 4
            + [
                vmem(large, F32), vmem((many, 2 * SPAN), F32), vmem((many, 2 * SPAN), BF16),
                vmem(large, F32), vmem((many, 2 * SPAN), F32),
                vmem((8, 128), F32), vmem((n_dp - 1, 8, 128), F32),
                vmem((8, 128), F32), vmem((n_dp - 1, 8, 128), F32),
                vmem((8, width), F32), vmem((inner - 1, 8, width), F32),
                vmem((8, width), F32), vmem((outer - 1, 8, width), F32),
                dma((8,)), dma((2,)), dma((2,)), dma, dma,
                dma, dma, dma, dma, dma, dma, dma, dma,
            ],
            compiler_params=pltpu.CompilerParams(
                collective_id=0, has_side_effects=True, vmem_limit_bytes=58 * 1024 * 1024
            ),
        )(*args)
        return pl.pallas_call(
            write_back,
            out_shape=[jax.ShapeDtypeStruct(s, BF16) for s in out_shapes]
            + [jax.ShapeDtypeStruct((width,), F32)],
            in_specs=[pl.BlockSpec(memory_space=pl.ANY)] * 7,
            out_specs=[hbm] * 7,
            scratch_shapes=[dma((7,))],
        )(*[pltpu.with_memory_space_constraint(x, pltpu.VMEM) for x in results])

    return jax.shard_map(
        step,
        mesh=mesh,
        in_specs=(P("seq", "dp"),) * 7 + (P("dp"),),
        out_specs=(P("seq", "dp"),) * 6 + (P("dp"),),
        check_vma=False,
    )
```

```python
import functools

import jax
import jax.numpy as jnp
from jax import lax
from jax.experimental import pallas as pl
from jax.experimental.pallas import tpu as pltpu
from jax.sharding import PartitionSpec as P

HD = 128
SPAN = 64
MEM = 256
NORM_EPS = 1e-05
SCALE = HD ** (-0.5)
MESH = pl.DeviceIdType.MESH
F32 = jnp.float32
BF16 = jnp.bfloat16


def nt(a, b):
    return lax.dot_general(a, b, (((1,), (1,)), ((), ())), preferred_element_type=F32)


def nn(a, b):
    return lax.dot_general(a, b, (((1,), (0,)), ((), ())), preferred_element_type=F32)


def tn(a, b):
    return lax.dot_general(a, b, (((0,), (0,)), ((), ())), preferred_element_type=F32)


def two_heads(x):
    first = lax.broadcasted_iota(jnp.int32, x.shape, 1) < HD
    zero = jnp.zeros_like(x)
    return jnp.concatenate([jnp.where(first, x, zero), jnp.where(first, zero, x)], axis=0)


def diagonal(x):
    first = lax.broadcasted_iota(jnp.int32, (SPAN, 2 * HD), 1) < HD
    return jnp.where(first, x[:SPAN], x[SPAN:])


def half_sums(x, left):
    zero = jnp.zeros_like(x)
    first = jnp.sum(jnp.where(left, x, zero), axis=1, keepdims=True)
    last = jnp.sum(jnp.where(left, zero, x), axis=1, keepdims=True)
    return first, last


def kernel(
    n_seq, n_dp, split, sq_h, og_h, nk_h, ns_h, eq_h, sk_h, sv_h, gain_h,
    qg, kg, sg, eqg, skg, svg, gg,
    sq, og, nk, ns, eq, sk, sv, gain,
    next_q, next_g, dq_out, dq_in, enc, enc_w, enc_low, val, weights,
    square_out, square_in, dot_out, dot_in, gain_out, gain_in,
    in_sem, halo_send, halo_recv, back_send, back_recv,
    square_send, square_recv, dot_send, dot_recv, gain_send, gain_recv,
):
    seq, dp = lax.axis_index("seq"), lax.axis_index("dp")
    before = lax.rem(seq + n_seq - 1, n_seq)
    after = lax.rem(seq + 1, n_seq)
    width = n_dp * 2 * HD

    far = sorted(range(1, n_dp), key=lambda k: -min(k, n_dp - k))
    dp_peers = [(seq, lax.rem(dp + k, n_dp)) for k in far]
    b_size, x_size, c_size = split
    block, rest = lax.div(seq, x_size * c_size), lax.rem(seq, x_size * c_size)
    across, core = lax.div(rest, c_size), lax.rem(rest, c_size)
    offsets = [(i, j, k) for i in range(b_size) for j in range(x_size) for k in range(c_size)][1:]
    offsets.sort(key=lambda o: -(4 * min(o[0], b_size - o[0]) + 2 * min(o[1], x_size - o[1]) + o[2]))
    seq_peers = [
        (lax.rem(block + i, b_size) * (x_size * c_size) + lax.rem(across + j, x_size) * c_size + lax.rem(core + k, c_size), dp)
        for i, j, k in offsets
    ]

    loads = {}
    for k, (name, src, dst) in enumerate([
        ("eq", eq_h, eq), ("sk", sk_h, sk), ("sv", sv_h, sv), ("ns", ns_h, ns),
        ("sq", sq_h, sq), ("og", og_h, og), ("nk", nk_h, nk), ("gain", gain_h, gain),
    ]):
        loads[name] = pltpu.make_async_copy(src, dst, in_sem.at[k])
        loads[name].start()

    barrier = pltpu.get_barrier_semaphore()
    peers = seq_peers + dp_peers
    for peer in peers:
        pl.semaphore_signal(barrier, inc=1, device_id=peer, device_id_type=MESH)

    left = lax.broadcasted_iota(jnp.int32, (MEM, 2 * SPAN), 1) < SPAN
    tiles = 2 * MEM // 8
    pick = (
        lax.broadcasted_iota(jnp.int32, (tiles, 8, 128), 2)
        == lax.broadcasted_iota(jnp.int32, (tiles, 8, 128), 0)
    )
    def fold(x):
        return jnp.sum(x[:, :HD] + x[:, HD:], axis=1, keepdims=True)

    loads["eq"].wait()
    loads["sk"].wait()
    loads["sv"].wait()
    loads["ns"].wait()
    squares = []
    for c in range(2):
        rows = pl.ds(c * MEM, MEM)
        keys = two_heads(sk[pl.ds(c * SPAN, SPAN), :])
        values = two_heads(sv[pl.ds(c * SPAN, SPAN), :])
        e = jnp.exp(nt(eq[rows, :], keys) * SCALE)
        first, last = half_sums(e, left)
        w = e * jnp.where(left, 1.0 / first, 1.0 / last)
        low = w.astype(BF16)
        enc_w[rows, :] = w
        enc_low[rows, :] = low
        x = ns[rows, :].astype(F32) + nn(low, values)
        enc[rows, :] = x
        squares.append(fold(x * x))

    def packed(parts):
        whole = jnp.concatenate(parts, axis=0).reshape(tiles, 8, 1)
        return jnp.sum(jnp.where(pick, whole, 0.0), axis=0)

    def column(x):
        return jnp.sum(jnp.where(pick, x[None], 0.0), axis=2, keepdims=True).reshape(2 * MEM, 1)

    def exchange(mine, out, into, send, recv):
        out[...] = mine
        copies = [
            pltpu.make_async_remote_copy(
                src_ref=out, dst_ref=into.at[k], send_sem=send, recv_sem=recv,
                device_id=peer, device_id_type=MESH)
            for k, peer in enumerate(dp_peers)
        ]
        for copy in copies:
            copy.start()

    def gather(out, into, recv):
        pltpu.make_async_copy(into, into, recv).wait()
        return out[...] + jnp.sum(into[...], axis=0)

    squares = packed(squares)
    pl.semaphore_wait(barrier, len(peers))

    halo = [
        pltpu.make_async_remote_copy(
            src_ref=src.at[pl.ds(0, SPAN)], dst_ref=dst, send_sem=halo_send.at[k], recv_sem=halo_recv.at[k],
            device_id=(before, dp), device_id_type=MESH)
        for k, (src, dst) in enumerate([(sq_h, next_q), (og_h, next_g)])
    ]
    for copy in halo:
        copy.start()

    exchange(squares, square_out, square_in, square_send, square_recv)

    loads["sq"].wait()
    loads["og"].wait()
    loads["nk"].wait()
    loads["gain"].wait()
    gains = gain[...].reshape(1, 2 * HD)
    last_row = lax.broadcasted_iota(jnp.int32, (SPAN, 2 * HD), 0) == SPAN - 1

    def tokens(c):
        if c == 0:
            return (
                jnp.where(last_row, sq[:SPAN, :], sq[SPAN:, :]),
                jnp.where(last_row, og[:SPAN, :], og[SPAN:, :]),
            )
        there = seq < n_seq - 1
        zero = jnp.zeros((SPAN, 2 * HD), BF16)
        return (
            jnp.where(last_row, sq[SPAN:, :], jnp.where(there, next_q[...], zero)),
            jnp.where(last_row, og[SPAN:, :], jnp.where(there, next_g[...], zero)),
        )

    pairs, dots = [], []
    for c in range(2):
        rows = pl.ds(c * MEM, MEM)
        if c == 1:
            for copy in halo:
                copy.wait_recv()
        q, g = tokens(c)
        q, g = two_heads(q), two_heads(g)
        pairs.append((q, g))
        e = jnp.exp(nt(nk[rows, :], q) * SCALE)
        w = e * (1.0 / jnp.sum(e, axis=0, keepdims=True))
        weights[rows, :] = w
        v = nn(w.astype(BF16), g)
        val[rows, :] = v
        dots.append(fold(v * gains * enc[rows, :]))

    exchange(packed(dots), dot_out, dot_in, dot_send, dot_recv)
    inverse = lax.rsqrt(gather(square_out, square_in, square_recv) * (1.0 / width) + NORM_EPS)
    packed_inverse = inverse
    inverse = column(inverse)

    own = jnp.zeros((8, 2 * HD), F32)
    for c in range(2):
        rows = pl.ds(c * MEM, MEM)
        term = val[rows, :] * enc[rows, :] * inverse[c * MEM:(c + 1) * MEM]
        own = own + jnp.sum(term.reshape(MEM // 8, 8, 2 * HD), axis=0)
    own = jnp.sum(own, axis=0, keepdims=True)
    gain_out[...] = jnp.concatenate([own[:, :HD], own[:, HD:]], axis=0)
    sums = [
        pltpu.make_async_remote_copy(
            src_ref=gain_out, dst_ref=gain_in.at[k], send_sem=gain_send, recv_sem=gain_recv,
            device_id=peer, device_id_type=MESH)
        for k, peer in enumerate(seq_peers)
    ]
    for copy in sums:
        copy.start()

    d_query = [None, None]
    for c in (1, 0):
        rows = pl.ds(c * MEM, MEM)
        q, g = pairs[c]
        normed = (enc[rows, :] * inverse[c * MEM:(c + 1) * MEM] * gains).astype(BF16)
        w = weights[rows, :]
        d_w = nt(normed, g)
        delta = jnp.sum(w * d_w, axis=0, keepdims=True)
        d_s = (w * (d_w - delta) * SCALE).astype(BF16)
        d_query[c] = diagonal(tn(d_s, nk[rows, :])).astype(BF16)
        if c == 1:
            dq_out[...] = d_query[c]
            back = pltpu.make_async_remote_copy(
                src_ref=dq_out, dst_ref=dq_in, send_sem=back_send, recv_sem=back_recv,
                device_id=(after, dp), device_id_type=MESH)
            back.start()
        kg[rows, :] = nn(d_s, q).astype(BF16)

    grad_dot = gather(dot_out, dot_in, dot_recv)
    slope = column(grad_dot * packed_inverse * packed_inverse * packed_inverse * (1.0 / width))
    for c in range(2):
        rows = pl.ds(c * MEM, MEM)
        at = slice(c * MEM, (c + 1) * MEM)
        span = pl.ds(c * SPAN, SPAN)
        keys = two_heads(sk[span, :])
        values = two_heads(sv[span, :])
        s_grad = (inverse[at] * (val[rows, :] * gains) - enc[rows, :] * slope[at]).astype(BF16)
        sg[rows, :] = s_grad
        w = enc_w[rows, :]
        d_w = nt(s_grad, values)
        first, last = half_sums(w * d_w, left)
        d_s = (w * (d_w - jnp.where(left, first, last)) * SCALE).astype(BF16)
        eqg[rows, :] = nn(d_s, keys).astype(BF16)
        skg[span, :] = diagonal(tn(d_s, eq[rows, :])).astype(BF16)
        svg[span, :] = diagonal(tn(enc_low[rows, :], s_grad)).astype(BF16)

    back.wait_recv()
    come = jnp.where(seq > 0, dq_in[...], jnp.zeros((SPAN, 2 * HD), BF16))
    qg[:SPAN, :] = jnp.where(last_row, d_query[0], come)
    qg[SPAN:, :] = jnp.where(last_row, d_query[1], d_query[0])

    for copy in halo + [back]:
        copy.wait_send()
    for slots, sem in ((square_in, square_send), (dot_in, dot_send), (gain_in, gain_send)):
        pltpu.make_async_copy(slots, slots, sem).wait()

    total = gather(gain_out, gain_in, gain_recv)
    gg[...] = jnp.concatenate([total[0:1], total[1:2]], axis=1).reshape(2 * HD)


def write_back(*refs):
    sources, targets, sem = refs[:7], refs[7:14], refs[14]
    copies = [pltpu.make_async_copy(a, b, sem.at[k]) for k, (a, b) in enumerate(zip(sources, targets))]
    for copy in copies:
        copy.start()
    for copy in copies:
        copy.wait()


def solution(mesh):
    n_seq, n_dp = mesh.shape["seq"], mesh.shape["dp"]
    across = min(4, n_seq // 4)
    split = (n_seq // (2 * across), across, 2)

    def step(*args):
        rows, width = args[0].shape
        many = args[2].shape[0]
        small, large = (rows, width), (many, width)
        out_shapes = [small, large, large, large, small, small]
        vmem = pltpu.VMEM
        dma = pltpu.SemaphoreType.DMA
        hbm = pl.BlockSpec(memory_space=pltpu.HBM)
        on_chip = pl.BlockSpec(memory_space=pltpu.VMEM)
        results = pl.pallas_call(
            functools.partial(kernel, n_seq, n_dp, split),
            out_shape=[vmem(s, BF16) for s in out_shapes] + [vmem((width,), F32)],
            in_specs=[hbm] * 8,
            out_specs=[on_chip] * 7,
            scratch_shapes=[
                vmem(small, BF16), vmem(small, BF16), vmem(large, BF16), vmem(large, BF16),
                vmem(large, BF16), vmem(small, BF16), vmem(small, BF16), vmem((width,), F32),
            ]
            + [vmem((SPAN, width), BF16)] * 4
            + [
                vmem(large, F32), vmem((many, 2 * SPAN), F32), vmem((many, 2 * SPAN), BF16),
                vmem(large, F32), vmem((many, 2 * SPAN), F32),
                vmem((8, 128), F32), vmem((n_dp - 1, 8, 128), F32),
                vmem((8, 128), F32), vmem((n_dp - 1, 8, 128), F32),
                vmem((2, HD), F32), vmem((n_seq - 1, 2, HD), F32),
                dma((8,)), dma((2,)), dma((2,)), dma, dma,
                dma, dma, dma, dma, dma, dma,
            ],
            compiler_params=pltpu.CompilerParams(
                collective_id=0, has_side_effects=True, vmem_limit_bytes=58 * 1024 * 1024
            ),
        )(*args)
        return pl.pallas_call(
            write_back,
            out_shape=[jax.ShapeDtypeStruct(s, BF16) for s in out_shapes]
            + [jax.ShapeDtypeStruct((width,), F32)],
            in_specs=[pl.BlockSpec(memory_space=pl.ANY)] * 7,
            out_specs=[hbm] * 7,
            scratch_shapes=[dma((7,))],
        )(*[pltpu.with_memory_space_constraint(x, pltpu.VMEM) for x in results])

    return jax.shard_map(
        step,
        mesh=mesh,
        in_specs=(P("seq", "dp"),) * 7 + (P("dp"),),
        out_specs=(P("seq", "dp"),) * 6 + (P("dp"),),
        check_vma=False,
    )
```

```python
import functools

import jax
import jax.numpy as jnp
from jax import lax
from jax.experimental import pallas as pl
from jax.experimental.pallas import tpu as pltpu
from jax.sharding import PartitionSpec as P

HD = 128
SPAN = 64
MEM = 256
NORM_EPS = 1e-05
SCALE = HD ** (-0.5)
MESH = pl.DeviceIdType.MESH
F32 = jnp.float32
BF16 = jnp.bfloat16


def nt(a, b):
    return lax.dot_general(a, b, (((1,), (1,)), ((), ())), preferred_element_type=F32)


def nn(a, b):
    return lax.dot_general(a, b, (((1,), (0,)), ((), ())), preferred_element_type=F32)


def tn(a, b):
    return lax.dot_general(a, b, (((0,), (0,)), ((), ())), preferred_element_type=F32)


def two_heads(x):
    first = lax.broadcasted_iota(jnp.int32, x.shape, 1) < HD
    zero = jnp.zeros_like(x)
    return jnp.concatenate([jnp.where(first, x, zero), jnp.where(first, zero, x)], axis=0)


def diagonal(x):
    first = lax.broadcasted_iota(jnp.int32, (SPAN, 2 * HD), 1) < HD
    return jnp.where(first, x[:SPAN], x[SPAN:])


def half_sums(x, left):
    zero = jnp.zeros_like(x)
    first = jnp.sum(jnp.where(left, x, zero), axis=1, keepdims=True)
    last = jnp.sum(jnp.where(left, zero, x), axis=1, keepdims=True)
    return first, last


def kernel(
    n_seq, n_dp, sq_h, og_h, nk_h, ns_h, eq_h, sk_h, sv_h, gain_h,
    qg, kg, sg, eqg, skg, svg, gg,
    sq, og, nk, ns, eq, sk, sv, gain,
    next_q, next_g, dq_out, dq_in, enc, enc_w, enc_low, val, weights,
    square_out, square_in, dot_out, dot_in, gain_out, gain_in,
    in_sem, halo_send, halo_recv, back_send, back_recv,
    square_send, square_recv, dot_send, dot_recv, gain_send, gain_recv,
):
    seq, dp = lax.axis_index("seq"), lax.axis_index("dp")
    before = lax.rem(seq + n_seq - 1, n_seq)
    after = lax.rem(seq + 1, n_seq)
    width = n_dp * 2 * HD

    def falling(me, n):
        return [n - 1 - k - lax.div(me + k + 1, n) for k in range(n - 1)]

    def rising(me, n):
        above = [lax.div(me - k + n - 1, n) for k in range(n - 1)]
        return [(k + 1 - up, me - up) for k, up in enumerate(above)]

    dp_peers = [((seq, peer), slot) for peer, slot in rising(dp, n_dp)]
    seq_peers = [((peer, dp), slot) for peer, slot in rising(seq, n_seq)]

    loads = {}
    for k, (name, src, dst) in enumerate([
        ("eq", eq_h, eq), ("sk", sk_h, sk), ("sv", sv_h, sv), ("ns", ns_h, ns),
        ("sq", sq_h, sq), ("og", og_h, og), ("nk", nk_h, nk), ("gain", gain_h, gain),
    ]):
        loads[name] = pltpu.make_async_copy(src, dst, in_sem.at[k])
        loads[name].start()

    barrier = pltpu.get_barrier_semaphore()
    peers = [(seq, peer) for peer in falling(dp, n_dp)] + [(peer, dp) for peer in falling(seq, n_seq)]
    for peer in peers:
        pl.semaphore_signal(barrier, inc=1, device_id=peer, device_id_type=MESH)

    left = lax.broadcasted_iota(jnp.int32, (MEM, 2 * SPAN), 1) < SPAN
    tiles = 2 * MEM // 8
    pick = (
        lax.broadcasted_iota(jnp.int32, (tiles, 8, 128), 2)
        == lax.broadcasted_iota(jnp.int32, (tiles, 8, 128), 0)
    )
    def fold(x):
        return jnp.sum(x[:, :HD] + x[:, HD:], axis=1, keepdims=True)

    loads["eq"].wait()
    loads["sk"].wait()
    loads["sv"].wait()
    loads["ns"].wait()
    squares = []
    for c in range(2):
        rows = pl.ds(c * MEM, MEM)
        keys = two_heads(sk[pl.ds(c * SPAN, SPAN), :])
        values = two_heads(sv[pl.ds(c * SPAN, SPAN), :])
        e = jnp.exp(nt(eq[rows, :], keys) * SCALE)
        first, last = half_sums(e, left)
        w = e * jnp.where(left, 1.0 / first, 1.0 / last)
        low = w.astype(BF16)
        enc_w[rows, :] = w
        enc_low[rows, :] = low
        x = ns[rows, :].astype(F32) + nn(low, values)
        enc[rows, :] = x
        squares.append(fold(x * x))

    def packed(parts):
        whole = jnp.concatenate(parts, axis=0).reshape(tiles, 8, 1)
        return jnp.sum(jnp.where(pick, whole, 0.0), axis=0)

    def column(x):
        return jnp.sum(jnp.where(pick, x[None], 0.0), axis=2, keepdims=True).reshape(2 * MEM, 1)

    def exchange(mine, out, into, send, recv):
        out[...] = mine
        copies = [
            pltpu.make_async_remote_copy(
                src_ref=out, dst_ref=into.at[slot], send_sem=send, recv_sem=recv,
                device_id=peer, device_id_type=MESH)
            for peer, slot in dp_peers
        ]
        for copy in copies:
            copy.start()

    def gather(out, into, recv):
        pltpu.make_async_copy(into, into, recv).wait()
        return out[...] + jnp.sum(into[...], axis=0)

    squares = packed(squares)
    pl.semaphore_wait(barrier, len(peers))

    halo = [
        pltpu.make_async_remote_copy(
            src_ref=src.at[pl.ds(0, SPAN)], dst_ref=dst, send_sem=halo_send.at[k], recv_sem=halo_recv.at[k],
            device_id=(before, dp), device_id_type=MESH)
        for k, (src, dst) in enumerate([(sq_h, next_q), (og_h, next_g)])
    ]
    for copy in halo:
        copy.start()

    exchange(squares, square_out, square_in, square_send, square_recv)

    loads["sq"].wait()
    loads["og"].wait()
    loads["nk"].wait()
    loads["gain"].wait()
    gains = gain[...].reshape(1, 2 * HD)
    last_row = lax.broadcasted_iota(jnp.int32, (SPAN, 2 * HD), 0) == SPAN - 1

    def tokens(c):
        if c == 0:
            return (
                jnp.where(last_row, sq[:SPAN, :], sq[SPAN:, :]),
                jnp.where(last_row, og[:SPAN, :], og[SPAN:, :]),
            )
        there = seq < n_seq - 1
        zero = jnp.zeros((SPAN, 2 * HD), BF16)
        return (
            jnp.where(last_row, sq[SPAN:, :], jnp.where(there, next_q[...], zero)),
            jnp.where(last_row, og[SPAN:, :], jnp.where(there, next_g[...], zero)),
        )

    pairs, dots = [], []
    for c in range(2):
        rows = pl.ds(c * MEM, MEM)
        if c == 1:
            for copy in halo:
                copy.wait_recv()
        q, g = tokens(c)
        q, g = two_heads(q), two_heads(g)
        pairs.append((q, g))
        e = jnp.exp(nt(nk[rows, :], q) * SCALE)
        w = e * (1.0 / jnp.sum(e, axis=0, keepdims=True))
        weights[rows, :] = w
        v = nn(w.astype(BF16), g)
        val[rows, :] = v
        dots.append(fold(v * gains * enc[rows, :]))

    exchange(packed(dots), dot_out, dot_in, dot_send, dot_recv)
    inverse = lax.rsqrt(gather(square_out, square_in, square_recv) * (1.0 / width) + NORM_EPS)
    packed_inverse = inverse
    inverse = column(inverse)

    own = jnp.zeros((8, 2 * HD), F32)
    for c in range(2):
        rows = pl.ds(c * MEM, MEM)
        term = val[rows, :] * enc[rows, :] * inverse[c * MEM:(c + 1) * MEM]
        own = own + jnp.sum(term.reshape(MEM // 8, 8, 2 * HD), axis=0)
    own = jnp.sum(own, axis=0, keepdims=True)
    gain_out[...] = jnp.concatenate([own[:, :HD], own[:, HD:]], axis=0)
    sums = [
        pltpu.make_async_remote_copy(
            src_ref=gain_out, dst_ref=gain_in.at[slot], send_sem=gain_send, recv_sem=gain_recv,
            device_id=peer, device_id_type=MESH)
        for peer, slot in seq_peers
    ]
    for copy in sums:
        copy.start()

    d_query = [None, None]
    for c in (1, 0):
        rows = pl.ds(c * MEM, MEM)
        q, g = pairs[c]
        normed = (enc[rows, :] * inverse[c * MEM:(c + 1) * MEM] * gains).astype(BF16)
        w = weights[rows, :]
        d_w = nt(normed, g)
        delta = jnp.sum(w * d_w, axis=0, keepdims=True)
        d_s = (w * (d_w - delta) * SCALE).astype(BF16)
        d_query[c] = diagonal(tn(d_s, nk[rows, :])).astype(BF16)
        if c == 1:
            dq_out[...] = d_query[c]
            back = pltpu.make_async_remote_copy(
                src_ref=dq_out, dst_ref=dq_in, send_sem=back_send, recv_sem=back_recv,
                device_id=(after, dp), device_id_type=MESH)
            back.start()
        kg[rows, :] = nn(d_s, q).astype(BF16)

    grad_dot = gather(dot_out, dot_in, dot_recv)
    slope = column(grad_dot * packed_inverse * packed_inverse * packed_inverse * (1.0 / width))
    for c in range(2):
        rows = pl.ds(c * MEM, MEM)
        at = slice(c * MEM, (c + 1) * MEM)
        span = pl.ds(c * SPAN, SPAN)
        keys = two_heads(sk[span, :])
        values = two_heads(sv[span, :])
        s_grad = (inverse[at] * (val[rows, :] * gains) - enc[rows, :] * slope[at]).astype(BF16)
        sg[rows, :] = s_grad
        w = enc_w[rows, :]
        d_w = nt(s_grad, values)
        first, last = half_sums(w * d_w, left)
        d_s = (w * (d_w - jnp.where(left, first, last)) * SCALE).astype(BF16)
        eqg[rows, :] = nn(d_s, keys).astype(BF16)
        skg[span, :] = diagonal(tn(d_s, eq[rows, :])).astype(BF16)
        svg[span, :] = diagonal(tn(enc_low[rows, :], s_grad)).astype(BF16)

    back.wait_recv()
    come = jnp.where(seq > 0, dq_in[...], jnp.zeros((SPAN, 2 * HD), BF16))
    qg[:SPAN, :] = jnp.where(last_row, d_query[0], come)
    qg[SPAN:, :] = jnp.where(last_row, d_query[1], d_query[0])

    for copy in halo + [back]:
        copy.wait_send()
    for slots, sem in ((square_in, square_send), (dot_in, dot_send), (gain_in, gain_send)):
        pltpu.make_async_copy(slots, slots, sem).wait()

    total = gather(gain_out, gain_in, gain_recv)
    gg[...] = jnp.concatenate([total[0:1], total[1:2]], axis=1).reshape(2 * HD)


def write_back(*refs):
    sources, targets, sem = refs[:7], refs[7:14], refs[14]
    copies = [pltpu.make_async_copy(a, b, sem.at[k]) for k, (a, b) in enumerate(zip(sources, targets))]
    for copy in copies:
        copy.start()
    for copy in copies:
        copy.wait()


def solution(mesh):
    n_seq, n_dp = mesh.shape["seq"], mesh.shape["dp"]
    def step(*args):
        rows, width = args[0].shape
        many = args[2].shape[0]
        small, large = (rows, width), (many, width)
        out_shapes = [small, large, large, large, small, small]
        vmem = pltpu.VMEM
        dma = pltpu.SemaphoreType.DMA
        hbm = pl.BlockSpec(memory_space=pltpu.HBM)
        on_chip = pl.BlockSpec(memory_space=pltpu.VMEM)
        results = pl.pallas_call(
            functools.partial(kernel, n_seq, n_dp),
            out_shape=[vmem(s, BF16) for s in out_shapes] + [vmem((width,), F32)],
            in_specs=[hbm] * 8,
            out_specs=[on_chip] * 7,
            scratch_shapes=[
                vmem(small, BF16), vmem(small, BF16), vmem(large, BF16), vmem(large, BF16),
                vmem(large, BF16), vmem(small, BF16), vmem(small, BF16), vmem((width,), F32),
            ]
            + [vmem((SPAN, width), BF16)] * 4
            + [
                vmem(large, F32), vmem((many, 2 * SPAN), F32), vmem((many, 2 * SPAN), BF16),
                vmem(large, F32), vmem((many, 2 * SPAN), F32),
                vmem((8, 128), F32), vmem((n_dp - 1, 8, 128), F32),
                vmem((8, 128), F32), vmem((n_dp - 1, 8, 128), F32),
                vmem((2, HD), F32), vmem((n_seq - 1, 2, HD), F32),
                dma((8,)), dma((2,)), dma((2,)), dma, dma,
                dma, dma, dma, dma, dma, dma,
            ],
            compiler_params=pltpu.CompilerParams(
                collective_id=0, has_side_effects=True, vmem_limit_bytes=58 * 1024 * 1024
            ),
        )(*args)
        return pl.pallas_call(
            write_back,
            out_shape=[jax.ShapeDtypeStruct(s, BF16) for s in out_shapes]
            + [jax.ShapeDtypeStruct((width,), F32)],
            in_specs=[pl.BlockSpec(memory_space=pl.ANY)] * 7,
            out_specs=[hbm] * 7,
            scratch_shapes=[dma((7,))],
        )(*[pltpu.with_memory_space_constraint(x, pltpu.VMEM) for x in results])

    return jax.shard_map(
        step,
        mesh=mesh,
        in_specs=(P("seq", "dp"),) * 7 + (P("dp"),),
        out_specs=(P("seq", "dp"),) * 6 + (P("dp"),),
        check_vma=False,
    )
```

```python
import functools

import jax
import jax.numpy as jnp
from jax import lax
from jax.experimental import pallas as pl
from jax.experimental.pallas import tpu as pltpu
from jax.sharding import PartitionSpec as P

HD = 128
SPAN = 64
MEM = 256
NORM_EPS = 1e-05
SCALE = HD ** (-0.5)
MESH = pl.DeviceIdType.MESH
HUB = 1
F32 = jnp.float32
BF16 = jnp.bfloat16


def nt(a, b):
    return lax.dot_general(a, b, (((1,), (1,)), ((), ())), preferred_element_type=F32)


def nn(a, b):
    return lax.dot_general(a, b, (((1,), (0,)), ((), ())), preferred_element_type=F32)


def tn(a, b):
    return lax.dot_general(a, b, (((0,), (0,)), ((), ())), preferred_element_type=F32)


def two_heads(x):
    first = lax.broadcasted_iota(jnp.int32, x.shape, 1) < HD
    zero = jnp.zeros_like(x)
    return jnp.concatenate([jnp.where(first, x, zero), jnp.where(first, zero, x)], axis=0)


def diagonal(x):
    first = lax.broadcasted_iota(jnp.int32, (SPAN, 2 * HD), 1) < HD
    return jnp.where(first, x[:SPAN], x[SPAN:])


def half_sums(x, left):
    zero = jnp.zeros_like(x)
    first = jnp.sum(jnp.where(left, x, zero), axis=1, keepdims=True)
    last = jnp.sum(jnp.where(left, zero, x), axis=1, keepdims=True)
    return first, last


def kernel(
    n_seq, n_dp, n_add, sq_h, og_h, nk_h, ns_h, eq_h, sk_h, sv_h, gain_h,
    qg, kg, sg, eqg, skg, svg, gg,
    sq, og, nk, ns, eq, sk, sv, gain,
    next_q, next_g, dq_out, dq_in, enc, enc_w, enc_low, val, weights,
    square_out, square_in, square_sum, dot_out, dot_in, dot_sum, gain_out, gain_in,
    in_sem, halo_send, halo_recv, back_send, back_recv,
    square_send, square_recv, square_send2, square_recv2, dot_send, dot_recv, dot_send2, dot_recv2, here, all_here, gain_send, gain_recv,
):
    seq, dp = lax.axis_index("seq"), lax.axis_index("dp")
    before = lax.rem(seq + n_seq - 1, n_seq)
    after = lax.rem(seq + 1, n_seq)
    width = n_dp * 2 * HD

    def rising(me, n):
        above = [lax.div(me - k + n - 1, n) for k in range(n - 1)]
        return [(k + 1 - up, me - up) for k, up in enumerate(above)]

    dp_peers = [(seq, peer) for peer, _ in rising(dp, n_dp)]
    seq_peers = [((peer, dp), slot) for peer, slot in rising(seq, n_seq)]
    adds = dp < n_add
    is_hub = seq == HUB

    loads = {}
    for k, (name, src, dst) in enumerate([
        ("eq", eq_h, eq), ("sk", sk_h, sk), ("sv", sv_h, sv), ("ns", ns_h, ns),
        ("sq", sq_h, sq), ("og", og_h, og), ("nk", nk_h, nk), ("gain", gain_h, gain),
    ]):
        loads[name] = pltpu.make_async_copy(src, dst, in_sem.at[k])
        loads[name].start()

    barrier = pltpu.get_barrier_semaphore()

    def greet(peers):
        for peer in peers:
            pl.semaphore_signal(barrier, inc=1, device_id=peer, device_id_type=MESH)

    greet([(before, dp), (after, dp)])

    @pl.when(adds)
    def _():
        greet(dp_peers)

    @pl.when(is_hub)
    def _():
        greet([peer for peer, _ in seq_peers])

    left = lax.broadcasted_iota(jnp.int32, (MEM, 2 * SPAN), 1) < SPAN
    tiles = 2 * MEM // 8
    pick = (
        lax.broadcasted_iota(jnp.int32, (tiles, 8, 128), 2)
        == lax.broadcasted_iota(jnp.int32, (tiles, 8, 128), 0)
    )
    def fold(x):
        return jnp.sum(x[:, :HD] + x[:, HD:], axis=1, keepdims=True)

    loads["eq"].wait()
    loads["sk"].wait()
    loads["sv"].wait()
    loads["ns"].wait()
    squares = []
    for c in range(2):
        rows = pl.ds(c * MEM, MEM)
        keys = two_heads(sk[pl.ds(c * SPAN, SPAN), :])
        values = two_heads(sv[pl.ds(c * SPAN, SPAN), :])
        e = jnp.exp(nt(eq[rows, :], keys) * SCALE)
        first, last = half_sums(e, left)
        w = e * jnp.where(left, 1.0 / first, 1.0 / last)
        low = w.astype(BF16)
        enc_w[rows, :] = w
        enc_low[rows, :] = low
        x = ns[rows, :].astype(F32) + nn(low, values)
        enc[rows, :] = x
        squares.append(fold(x * x))

    def packed(parts):
        whole = jnp.concatenate(parts, axis=0).reshape(tiles, 8, 1)
        return jnp.sum(jnp.where(pick, whole, 0.0), axis=0)

    def column(x):
        return jnp.sum(jnp.where(pick, x[None], 0.0), axis=2, keepdims=True).reshape(2 * MEM, 1)

    def parts(out, into, send, recv, act):
        for k in range(n_add):
            @pl.when(dp != k)
            def _():
                act(pltpu.make_async_remote_copy(
                    src_ref=out, dst_ref=into.at[dp - jnp.where(dp > k, 1, 0)], send_sem=send, recv_sem=recv,
                    device_id=(seq, k), device_id_type=MESH))

    def answers(total, send, recv, act):
        for k in range(1, n_dp // n_add):
            act(pltpu.make_async_remote_copy(
                src_ref=total, dst_ref=total, send_sem=send, recv_sem=recv,
                device_id=(seq, dp + k * n_add), device_id_type=MESH))

    def begin(copy):
        copy.start()

    def left_here(copy):
        copy.wait_send()

    def exchange(mine, out, into, send, recv):
        out[...] = mine
        parts(out, into, send, recv, begin)

    def gather(out, into, recv, total, total_send, total_recv):
        @pl.when(adds)
        def _():
            pltpu.make_async_copy(into, into, recv).wait()
            total[...] = out[...] + jnp.sum(into[...], axis=0)
            answers(total, total_send, total_recv, begin)

        @pl.when(jnp.logical_not(adds))
        def _():
            pltpu.make_async_copy(total, total, total_recv).wait()

        return total[...]

    squares = packed(squares)
    pl.semaphore_wait(barrier, 2 + n_add - jnp.where(adds, 1, 0) + jnp.where(is_hub, 0, 1))

    halo = [
        pltpu.make_async_remote_copy(
            src_ref=src.at[pl.ds(0, SPAN)], dst_ref=dst, send_sem=halo_send.at[k], recv_sem=halo_recv.at[k],
            device_id=(before, dp), device_id_type=MESH)
        for k, (src, dst) in enumerate([(sq_h, next_q), (og_h, next_g)])
    ]
    for copy in halo:
        copy.start()

    exchange(squares, square_out, square_in, square_send, square_recv)

    @pl.when(jnp.logical_not(is_hub))
    def _():
        pl.semaphore_signal(here, inc=1, device_id=(HUB, dp), device_id_type=MESH)


    loads["sq"].wait()
    loads["og"].wait()
    loads["nk"].wait()
    loads["gain"].wait()
    gains = gain[...].reshape(1, 2 * HD)
    last_row = lax.broadcasted_iota(jnp.int32, (SPAN, 2 * HD), 0) == SPAN - 1

    def tokens(c):
        if c == 0:
            return (
                jnp.where(last_row, sq[:SPAN, :], sq[SPAN:, :]),
                jnp.where(last_row, og[:SPAN, :], og[SPAN:, :]),
            )
        there = seq < n_seq - 1
        zero = jnp.zeros((SPAN, 2 * HD), BF16)
        return (
            jnp.where(last_row, sq[SPAN:, :], jnp.where(there, next_q[...], zero)),
            jnp.where(last_row, og[SPAN:, :], jnp.where(there, next_g[...], zero)),
        )

    pairs, dots = [], []
    for c in range(2):
        rows = pl.ds(c * MEM, MEM)
        if c == 1:
            @pl.when(is_hub)
            def _():
                pl.semaphore_wait(here, n_seq - 1)
                for peer, _ in seq_peers:
                    pl.semaphore_signal(all_here, inc=1, device_id=peer, device_id_type=MESH)

            for copy in halo:
                copy.wait_recv()
        q, g = tokens(c)
        q, g = two_heads(q), two_heads(g)
        pairs.append((q, g))
        e = jnp.exp(nt(nk[rows, :], q) * SCALE)
        w = e * (1.0 / jnp.sum(e, axis=0, keepdims=True))
        weights[rows, :] = w
        v = nn(w.astype(BF16), g)
        val[rows, :] = v
        dots.append(fold(v * gains * enc[rows, :]))

    exchange(packed(dots), dot_out, dot_in, dot_send, dot_recv)
    inverse = lax.rsqrt(gather(square_out, square_in, square_recv, square_sum, square_send2, square_recv2) * (1.0 / width) + NORM_EPS)
    packed_inverse = inverse
    inverse = column(inverse)

    own = jnp.zeros((8, 2 * HD), F32)
    for c in range(2):
        rows = pl.ds(c * MEM, MEM)
        term = val[rows, :] * enc[rows, :] * inverse[c * MEM:(c + 1) * MEM]
        own = own + jnp.sum(term.reshape(MEM // 8, 8, 2 * HD), axis=0)
    own = jnp.sum(own, axis=0, keepdims=True)
    gain_out[...] = jnp.concatenate([own[:, :HD], own[:, HD:]], axis=0)
    @pl.when(jnp.logical_not(is_hub))
    def _():
        pl.semaphore_wait(all_here, 1)

    sums = [
        pltpu.make_async_remote_copy(
            src_ref=gain_out, dst_ref=gain_in.at[slot], send_sem=gain_send, recv_sem=gain_recv,
            device_id=peer, device_id_type=MESH)
        for peer, slot in seq_peers
    ]
    for copy in sums:
        copy.start()

    d_query = [None, None]
    for c in (1, 0):
        rows = pl.ds(c * MEM, MEM)
        q, g = pairs[c]
        normed = (enc[rows, :] * inverse[c * MEM:(c + 1) * MEM] * gains).astype(BF16)
        w = weights[rows, :]
        d_w = nt(normed, g)
        delta = jnp.sum(w * d_w, axis=0, keepdims=True)
        d_s = (w * (d_w - delta) * SCALE).astype(BF16)
        d_query[c] = diagonal(tn(d_s, nk[rows, :])).astype(BF16)
        if c == 1:
            dq_out[...] = d_query[c]
            back = pltpu.make_async_remote_copy(
                src_ref=dq_out, dst_ref=dq_in, send_sem=back_send, recv_sem=back_recv,
                device_id=(after, dp), device_id_type=MESH)
            back.start()
        kg[rows, :] = nn(d_s, q).astype(BF16)

    grad_dot = gather(dot_out, dot_in, dot_recv, dot_sum, dot_send2, dot_recv2)
    slope = column(grad_dot * packed_inverse * packed_inverse * packed_inverse * (1.0 / width))
    for c in range(2):
        rows = pl.ds(c * MEM, MEM)
        at = slice(c * MEM, (c + 1) * MEM)
        span = pl.ds(c * SPAN, SPAN)
        keys = two_heads(sk[span, :])
        values = two_heads(sv[span, :])
        s_grad = (inverse[at] * (val[rows, :] * gains) - enc[rows, :] * slope[at]).astype(BF16)
        sg[rows, :] = s_grad
        w = enc_w[rows, :]
        d_w = nt(s_grad, values)
        first, last = half_sums(w * d_w, left)
        d_s = (w * (d_w - jnp.where(left, first, last)) * SCALE).astype(BF16)
        eqg[rows, :] = nn(d_s, keys).astype(BF16)
        skg[span, :] = diagonal(tn(d_s, eq[rows, :])).astype(BF16)
        svg[span, :] = diagonal(tn(enc_low[rows, :], s_grad)).astype(BF16)

    back.wait_recv()
    come = jnp.where(seq > 0, dq_in[...], jnp.zeros((SPAN, 2 * HD), BF16))
    qg[:SPAN, :] = jnp.where(last_row, d_query[0], come)
    qg[SPAN:, :] = jnp.where(last_row, d_query[1], d_query[0])

    for copy in halo + [back]:
        copy.wait_send()
    parts(square_out, square_in, square_send, square_recv, left_here)
    parts(dot_out, dot_in, dot_send, dot_recv, left_here)

    @pl.when(adds)
    def _():
        answers(square_sum, square_send2, square_recv2, left_here)
        answers(dot_sum, dot_send2, dot_recv2, left_here)

    pltpu.make_async_copy(gain_in, gain_in, gain_send).wait()
    pltpu.make_async_copy(gain_in, gain_in, gain_recv).wait()
    total = gain_out[...] + jnp.sum(gain_in[...], axis=0)
    gg[...] = jnp.concatenate([total[0:1], total[1:2]], axis=1).reshape(2 * HD)


def write_back(*refs):
    sources, targets, sem = refs[:7], refs[7:14], refs[14]
    copies = [pltpu.make_async_copy(a, b, sem.at[k]) for k, (a, b) in enumerate(zip(sources, targets))]
    for copy in copies:
        copy.start()
    for copy in copies:
        copy.wait()


def solution(mesh):
    n_seq, n_dp = mesh.shape["seq"], mesh.shape["dp"]
    def step(*args):
        rows, width = args[0].shape
        many = args[2].shape[0]
        small, large = (rows, width), (many, width)
        out_shapes = [small, large, large, large, small, small]
        vmem = pltpu.VMEM
        dma = pltpu.SemaphoreType.DMA
        hbm = pl.BlockSpec(memory_space=pltpu.HBM)
        on_chip = pl.BlockSpec(memory_space=pltpu.VMEM)
        results = pl.pallas_call(
            functools.partial(kernel, n_seq, n_dp, min(4, n_dp // 2)),
            out_shape=[vmem(s, BF16) for s in out_shapes] + [vmem((width,), F32)],
            in_specs=[hbm] * 8,
            out_specs=[on_chip] * 7,
            scratch_shapes=[
                vmem(small, BF16), vmem(small, BF16), vmem(large, BF16), vmem(large, BF16),
                vmem(large, BF16), vmem(small, BF16), vmem(small, BF16), vmem((width,), F32),
            ]
            + [vmem((SPAN, width), BF16)] * 4
            + [
                vmem(large, F32), vmem((many, 2 * SPAN), F32), vmem((many, 2 * SPAN), BF16),
                vmem(large, F32), vmem((many, 2 * SPAN), F32),
                vmem((8, 128), F32), vmem((n_dp - 1, 8, 128), F32), vmem((8, 128), F32),
                vmem((8, 128), F32), vmem((n_dp - 1, 8, 128), F32), vmem((8, 128), F32),
                vmem((2, HD), F32), vmem((n_seq - 1, 2, HD), F32),
                dma((8,)), dma((2,)), dma((2,)), dma, dma,
                dma, dma, dma, dma, dma, dma, dma, dma,
                pltpu.SemaphoreType.REGULAR, pltpu.SemaphoreType.REGULAR, dma, dma,
            ],
            compiler_params=pltpu.CompilerParams(
                collective_id=0, has_side_effects=True, vmem_limit_bytes=58 * 1024 * 1024
            ),
        )(*args)
        return pl.pallas_call(
            write_back,
            out_shape=[jax.ShapeDtypeStruct(s, BF16) for s in out_shapes]
            + [jax.ShapeDtypeStruct((width,), F32)],
            in_specs=[pl.BlockSpec(memory_space=pl.ANY)] * 7,
            out_specs=[hbm] * 7,
            scratch_shapes=[dma((7,))],
        )(*[pltpu.with_memory_space_constraint(x, pltpu.VMEM) for x in results])

    return jax.shard_map(
        step,
        mesh=mesh,
        in_specs=(P("seq", "dp"),) * 7 + (P("dp"),),
        out_specs=(P("seq", "dp"),) * 6 + (P("dp"),),
        check_vma=False,
    )
```

```python
import functools

import jax
import jax.numpy as jnp
from jax import lax
from jax.experimental import pallas as pl
from jax.experimental.pallas import tpu as pltpu
from jax.sharding import PartitionSpec as P

HD = 128
SPAN = 64
MEM = 256
NORM_EPS = 1e-05
SCALE = HD ** (-0.5)
MESH = pl.DeviceIdType.MESH
HUB = 1
F32 = jnp.float32
BF16 = jnp.bfloat16


def nt(a, b):
    return lax.dot_general(a, b, (((1,), (1,)), ((), ())), preferred_element_type=F32)


def nn(a, b):
    return lax.dot_general(a, b, (((1,), (0,)), ((), ())), preferred_element_type=F32)


def tn(a, b):
    return lax.dot_general(a, b, (((0,), (0,)), ((), ())), preferred_element_type=F32)


def two_heads(x):
    first = lax.broadcasted_iota(jnp.int32, x.shape, 1) < HD
    zero = jnp.zeros_like(x)
    return jnp.concatenate([jnp.where(first, x, zero), jnp.where(first, zero, x)], axis=0)


def diagonal(x):
    first = lax.broadcasted_iota(jnp.int32, (SPAN, 2 * HD), 1) < HD
    return jnp.where(first, x[:SPAN], x[SPAN:])


def half_sums(x, left):
    zero = jnp.zeros_like(x)
    first = jnp.sum(jnp.where(left, x, zero), axis=1, keepdims=True)
    last = jnp.sum(jnp.where(left, zero, x), axis=1, keepdims=True)
    return first, last


def kernel(
    n_seq, n_dp, n_add, sq_h, og_h, nk_h, ns_h, eq_h, sk_h, sv_h, gain_h,
    qg, kg, sg, eqg, skg, svg, gg,
    sq, og, nk, ns, eq, sk, sv, gain,
    next_q, next_g, dq_out, dq_in, enc, enc_w, enc_low, val, weights,
    square_out, square_in, square_sum, dot_out, dot_in, dot_sum, gain_out, gain_in,
    in_sem, halo_send, halo_recv, back_send, back_recv,
    square_send, square_recv, square_send2, square_recv2, dot_send, dot_recv, dot_send2, dot_recv2, here, all_here, gain_send, gain_recv,
):
    seq, dp = lax.axis_index("seq"), lax.axis_index("dp")
    before = lax.rem(seq + n_seq - 1, n_seq)
    after = lax.rem(seq + 1, n_seq)
    width = n_dp * 2 * HD

    def rising(me, n):
        above = [lax.div(me - k + n - 1, n) for k in range(n - 1)]
        return [(k + 1 - up, me - up) for k, up in enumerate(above)]

    dp_peers = [(seq, peer) for peer, _ in rising(dp, n_dp)]
    seq_peers = [((peer, dp), slot) for peer, slot in rising(seq, n_seq)]
    adds = dp < n_add
    is_hub = seq == HUB

    loads = {}
    for k, (name, src, dst) in enumerate([
        ("eq", eq_h, eq), ("sk", sk_h, sk), ("sv", sv_h, sv), ("ns", ns_h, ns),
        ("sq", sq_h, sq), ("og", og_h, og), ("nk", nk_h, nk), ("gain", gain_h, gain),
    ]):
        loads[name] = pltpu.make_async_copy(src, dst, in_sem.at[k])
        loads[name].start()

    barrier = pltpu.get_barrier_semaphore()

    def greet(peers):
        for peer in peers:
            pl.semaphore_signal(barrier, inc=1, device_id=peer, device_id_type=MESH)

    greet([(before, dp), (after, dp)])

    @pl.when(adds)
    def _():
        greet(dp_peers)

    @pl.when(is_hub)
    def _():
        greet([peer for peer, _ in seq_peers])

    left = lax.broadcasted_iota(jnp.int32, (MEM, 2 * SPAN), 1) < SPAN
    tiles = 2 * MEM // 8
    pick = (
        lax.broadcasted_iota(jnp.int32, (tiles, 8, 128), 2)
        == lax.broadcasted_iota(jnp.int32, (tiles, 8, 128), 0)
    )
    def fold(x):
        return jnp.sum(x[:, :HD] + x[:, HD:], axis=1, keepdims=True)

    loads["eq"].wait()
    loads["sk"].wait()
    squares = []
    for c in range(2):
        rows = pl.ds(c * MEM, MEM)
        keys = two_heads(sk[pl.ds(c * SPAN, SPAN), :])
        e = jnp.exp(nt(eq[rows, :], keys) * SCALE)
        first, last = half_sums(e, left)
        w = e * jnp.where(left, 1.0 / first, 1.0 / last)
        low = w.astype(BF16)
        if c == 0:
            loads["sv"].wait()
            loads["ns"].wait()
        values = two_heads(sv[pl.ds(c * SPAN, SPAN), :])
        enc_w[rows, :] = w
        enc_low[rows, :] = low
        x = ns[rows, :].astype(F32) + nn(low, values)
        enc[rows, :] = x
        squares.append(fold(x * x))

    def packed(parts):
        whole = jnp.concatenate(parts, axis=0).reshape(tiles, 8, 1)
        return jnp.sum(jnp.where(pick, whole, 0.0), axis=0)

    def column(x):
        return jnp.sum(jnp.where(pick, x[None], 0.0), axis=2, keepdims=True).reshape(2 * MEM, 1)

    def parts(out, into, send, recv, act):
        for k in range(n_add):
            @pl.when(dp != k)
            def _():
                act(pltpu.make_async_remote_copy(
                    src_ref=out, dst_ref=into.at[dp - jnp.where(dp > k, 1, 0)], send_sem=send, recv_sem=recv,
                    device_id=(seq, k), device_id_type=MESH))

    def answers(total, send, recv, act):
        for k in range(1, n_dp // n_add):
            act(pltpu.make_async_remote_copy(
                src_ref=total, dst_ref=total, send_sem=send, recv_sem=recv,
                device_id=(seq, dp + k * n_add), device_id_type=MESH))

    def begin(copy):
        copy.start()

    def left_here(copy):
        copy.wait_send()

    def exchange(mine, out, into, send, recv):
        out[...] = mine
        parts(out, into, send, recv, begin)

    def gather(out, into, recv, total, total_send, total_recv):
        @pl.when(adds)
        def _():
            pltpu.make_async_copy(into, into, recv).wait()
            total[...] = out[...] + jnp.sum(into[...], axis=0)
            answers(total, total_send, total_recv, begin)

        @pl.when(jnp.logical_not(adds))
        def _():
            pltpu.make_async_copy(total, total, total_recv).wait()

        return total[...]

    squares = packed(squares)
    pl.semaphore_wait(barrier, 2 + n_add - jnp.where(adds, 1, 0) + jnp.where(is_hub, 0, 1))

    exchange(squares, square_out, square_in, square_send, square_recv)

    halo = [
        pltpu.make_async_remote_copy(
            src_ref=src.at[pl.ds(0, SPAN)], dst_ref=dst, send_sem=halo_send.at[k], recv_sem=halo_recv.at[k],
            device_id=(before, dp), device_id_type=MESH)
        for k, (src, dst) in enumerate([(sq_h, next_q), (og_h, next_g)])
    ]
    for copy in halo:
        copy.start()

    @pl.when(jnp.logical_not(is_hub))
    def _():
        pl.semaphore_signal(here, inc=1, device_id=(HUB, dp), device_id_type=MESH)


    loads["sq"].wait()
    loads["og"].wait()
    loads["nk"].wait()
    loads["gain"].wait()
    gains = gain[...].reshape(1, 2 * HD)
    last_row = lax.broadcasted_iota(jnp.int32, (SPAN, 2 * HD), 0) == SPAN - 1

    def tokens(c):
        if c == 0:
            return (
                jnp.where(last_row, sq[:SPAN, :], sq[SPAN:, :]),
                jnp.where(last_row, og[:SPAN, :], og[SPAN:, :]),
            )
        there = seq < n_seq - 1
        zero = jnp.zeros((SPAN, 2 * HD), BF16)
        return (
            jnp.where(last_row, sq[SPAN:, :], jnp.where(there, next_q[...], zero)),
            jnp.where(last_row, og[SPAN:, :], jnp.where(there, next_g[...], zero)),
        )

    pairs, dots = [], []
    for c in range(2):
        rows = pl.ds(c * MEM, MEM)
        if c == 1:
            @pl.when(is_hub)
            def _():
                pl.semaphore_wait(here, n_seq - 1)
                for peer, _ in seq_peers:
                    pl.semaphore_signal(all_here, inc=1, device_id=peer, device_id_type=MESH)

            for copy in halo:
                copy.wait_recv()
        q, g = tokens(c)
        q, g = two_heads(q), two_heads(g)
        pairs.append((q, g))
        e = jnp.exp(nt(nk[rows, :], q) * SCALE)
        w = e * (1.0 / jnp.sum(e, axis=0, keepdims=True))
        weights[rows, :] = w
        v = nn(w.astype(BF16), g)
        val[rows, :] = v
        dots.append(fold(v * gains * enc[rows, :]))

    exchange(packed(dots), dot_out, dot_in, dot_send, dot_recv)
    inverse = lax.rsqrt(gather(square_out, square_in, square_recv, square_sum, square_send2, square_recv2) * (1.0 / width) + NORM_EPS)
    packed_inverse = inverse
    inverse = column(inverse)

    own = jnp.zeros((8, 2 * HD), F32)
    for c in range(2):
        rows = pl.ds(c * MEM, MEM)
        term = val[rows, :] * enc[rows, :] * inverse[c * MEM:(c + 1) * MEM]
        own = own + jnp.sum(term.reshape(MEM // 8, 8, 2 * HD), axis=0)
    own = jnp.sum(own, axis=0, keepdims=True)
    gain_out[...] = jnp.concatenate([own[:, :HD], own[:, HD:]], axis=0)
    @pl.when(jnp.logical_not(is_hub))
    def _():
        pl.semaphore_wait(all_here, 1)

    sums = [
        pltpu.make_async_remote_copy(
            src_ref=gain_out, dst_ref=gain_in.at[slot], send_sem=gain_send, recv_sem=gain_recv,
            device_id=peer, device_id_type=MESH)
        for peer, slot in seq_peers
    ]
    for copy in sums:
        copy.start()

    d_query = [None, None]
    for c in (1, 0):
        rows = pl.ds(c * MEM, MEM)
        q, g = pairs[c]
        normed = (enc[rows, :] * inverse[c * MEM:(c + 1) * MEM] * gains).astype(BF16)
        w = weights[rows, :]
        d_w = nt(normed, g)
        delta = jnp.sum(w * d_w, axis=0, keepdims=True)
        d_s = (w * (d_w - delta) * SCALE).astype(BF16)
        d_query[c] = diagonal(tn(d_s, nk[rows, :])).astype(BF16)
        if c == 1:
            dq_out[...] = d_query[c]
            back = pltpu.make_async_remote_copy(
                src_ref=dq_out, dst_ref=dq_in, send_sem=back_send, recv_sem=back_recv,
                device_id=(after, dp), device_id_type=MESH)
            back.start()
        kg[rows, :] = nn(d_s, q).astype(BF16)

    grad_dot = gather(dot_out, dot_in, dot_recv, dot_sum, dot_send2, dot_recv2)
    slope = column(grad_dot * packed_inverse * packed_inverse * packed_inverse * (1.0 / width))
    for c in range(2):
        rows = pl.ds(c * MEM, MEM)
        at = slice(c * MEM, (c + 1) * MEM)
        span = pl.ds(c * SPAN, SPAN)
        keys = two_heads(sk[span, :])
        values = two_heads(sv[span, :])
        s_grad = (inverse[at] * (val[rows, :] * gains) - enc[rows, :] * slope[at]).astype(BF16)
        sg[rows, :] = s_grad
        w = enc_w[rows, :]
        d_w = nt(s_grad, values)
        first, last = half_sums(w * d_w, left)
        d_s = (w * (d_w - jnp.where(left, first, last)) * SCALE).astype(BF16)
        eqg[rows, :] = nn(d_s, keys).astype(BF16)
        skg[span, :] = diagonal(tn(d_s, eq[rows, :])).astype(BF16)
        svg[span, :] = diagonal(tn(enc_low[rows, :], s_grad)).astype(BF16)

    back.wait_recv()
    come = jnp.where(seq > 0, dq_in[...], jnp.zeros((SPAN, 2 * HD), BF16))
    qg[:SPAN, :] = jnp.where(last_row, d_query[0], come)
    qg[SPAN:, :] = jnp.where(last_row, d_query[1], d_query[0])

    for copy in halo + [back]:
        copy.wait_send()
    parts(square_out, square_in, square_send, square_recv, left_here)
    parts(dot_out, dot_in, dot_send, dot_recv, left_here)

    @pl.when(adds)
    def _():
        answers(square_sum, square_send2, square_recv2, left_here)
        answers(dot_sum, dot_send2, dot_recv2, left_here)

    pltpu.make_async_copy(gain_in, gain_in, gain_send).wait()
    pltpu.make_async_copy(gain_in, gain_in, gain_recv).wait()
    total = gain_out[...] + jnp.sum(gain_in[...], axis=0)
    gg[...] = jnp.concatenate([total[0:1], total[1:2]], axis=1).reshape(2 * HD)


def write_back(*refs):
    sources, targets, sem = refs[:7], refs[7:14], refs[14]
    copies = [pltpu.make_async_copy(a, b, sem.at[k]) for k, (a, b) in enumerate(zip(sources, targets))]
    for copy in copies:
        copy.start()
    for copy in copies:
        copy.wait()


def solution(mesh):
    n_seq, n_dp = mesh.shape["seq"], mesh.shape["dp"]
    def step(*args):
        rows, width = args[0].shape
        many = args[2].shape[0]
        small, large = (rows, width), (many, width)
        out_shapes = [small, large, large, large, small, small]
        vmem = pltpu.VMEM
        dma = pltpu.SemaphoreType.DMA
        hbm = pl.BlockSpec(memory_space=pltpu.HBM)
        on_chip = pl.BlockSpec(memory_space=pltpu.VMEM)
        results = pl.pallas_call(
            functools.partial(kernel, n_seq, n_dp, min(4, n_dp // 2)),
            out_shape=[vmem(s, BF16) for s in out_shapes] + [vmem((width,), F32)],
            in_specs=[hbm] * 8,
            out_specs=[on_chip] * 7,
            scratch_shapes=[
                vmem(small, BF16), vmem(small, BF16), vmem(large, BF16), vmem(large, BF16),
                vmem(large, BF16), vmem(small, BF16), vmem(small, BF16), vmem((width,), F32),
            ]
            + [vmem((SPAN, width), BF16)] * 4
            + [
                vmem(large, F32), vmem((many, 2 * SPAN), F32), vmem((many, 2 * SPAN), BF16),
                vmem(large, F32), vmem((many, 2 * SPAN), F32),
                vmem((8, 128), F32), vmem((n_dp - 1, 8, 128), F32), vmem((8, 128), F32),
                vmem((8, 128), F32), vmem((n_dp - 1, 8, 128), F32), vmem((8, 128), F32),
                vmem((2, HD), F32), vmem((n_seq - 1, 2, HD), F32),
                dma((8,)), dma((2,)), dma((2,)), dma, dma,
                dma, dma, dma, dma, dma, dma, dma, dma,
                pltpu.SemaphoreType.REGULAR, pltpu.SemaphoreType.REGULAR, dma, dma,
            ],
            compiler_params=pltpu.CompilerParams(
                collective_id=0, has_side_effects=True, vmem_limit_bytes=58 * 1024 * 1024
            ),
        )(*args)
        return pl.pallas_call(
            write_back,
            out_shape=[jax.ShapeDtypeStruct(s, BF16) for s in out_shapes]
            + [jax.ShapeDtypeStruct((width,), F32)],
            in_specs=[pl.BlockSpec(memory_space=pl.ANY)] * 7,
            out_specs=[hbm] * 7,
            scratch_shapes=[dma((7,))],
        )(*[pltpu.with_memory_space_constraint(x, pltpu.VMEM) for x in results])

    return jax.shard_map(
        step,
        mesh=mesh,
        in_specs=(P("seq", "dp"),) * 7 + (P("dp"),),
        out_specs=(P("seq", "dp"),) * 6 + (P("dp"),),
        check_vma=False,
    )
```
